256 devices in a mesh: outer: 16 (over z, y_hi), inner: 16 (over y_lo, x, core).
Axes of the slice: x: 4, y: 4 (y_hi: 2, y_lo: 2; y = y_hi * 2 + y_lo), z: 8, core: 2. Of those that a mesh axis runs over, the one named last changes fastest.
Arguments:
- queries: bfloat16 [32768, 32, 128], P(('outer', 'inner')), may hold values from -6 to 6
- keys: bfloat16 [32768, 4, 128], P(('outer', 'inner')), may hold values from -6 to 6
- values: bfloat16 [32768, 4, 128], P(('outer', 'inner')), may hold values from -6 to 6
- output_gradient: bfloat16 [32768, 32, 128], P(('outer', 'inner')), may hold values from -6 to 6
- kept_offset: int32 [256, 128], replicated, may hold values from 0 to 1024, as said below
- region_pos: int32 [256], replicated, may hold values from 0 to 255, each once
Outputs:
- attn_out: bfloat16 [32768, 32, 128], P(('outer', 'inner'))
- grad_queries: bfloat16 [32768, 32, 128], P(('outer', 'inner'))
- key_gradient: bfloat16 [32768, 4, 128], P(('outer', 'inner'))
- value_gradient: bfloat16 [32768, 4, 128], P(('outer', 'inner'))
The draws below stay inside these ranges and needn't reach their ends.
Inputs may be any that keep to these rules, and one draw needn't show every extreme that they name: In each row of kept_offset the live slots (values under 1024) come first and strictly increase; the remaining slots hold 1024. Every shard has at least two live slots, some shard has all 128 live with offset 0 in its first slot, and some shard has empty slots.
All inputs are finite; a program needn't handle non-finite values.
Results may differ from the reference program's by a relative error of at most 0.025.
Values may be sent and summed in bfloat16 or wider, within the bound.
No kernel may reach another device: no remote copies, remote signals or barrier semaphores. Data moves between devices by JAX's collectives and lax.ppermute only.
A program may use at most 128 MiB of HBM per device.

```python
import jax
import jax.numpy as jnp
from jax import lax

QUERY_HEADS = 32
KEY_VALUE_HEADS = 4
HEAD_SIZE = 128
REGION = 1024
KEPT_SLOTS = 128
SEQUENCE_SHARDS = 256
TOKEN_SLOTS = 32768
N_OUTER = 16
N_INNER = 16


def draw_queries(key, part):
    key = jax.random.fold_in(key, 11)
    array_shape = (SEQUENCE_SHARDS, KEPT_SLOTS, KEY_VALUE_HEADS, QUERY_HEADS // KEY_VALUE_HEADS, HEAD_SIZE)
    entry_list = jnp.clip(jax.random.normal(key, array_shape, jnp.float32), -6.0, 6.0)
    return entry_list.reshape(TOKEN_SLOTS, QUERY_HEADS, HEAD_SIZE).astype(jnp.bfloat16)


def draw_keys(key, part):
    key = jax.random.fold_in(key, 23)
    array_shape = (SEQUENCE_SHARDS, KEPT_SLOTS, KEY_VALUE_HEADS, HEAD_SIZE)
    entry_list = jnp.clip(jax.random.normal(key, array_shape, jnp.float32), -6.0, 6.0)
    return entry_list.reshape(TOKEN_SLOTS, KEY_VALUE_HEADS, HEAD_SIZE).astype(jnp.bfloat16)


def draw_kept_offset(key, part):
    key = jax.random.fold_in(key, 37)
    count_key, full_key, place_key = jax.random.split(key, 3)
    lowest = max(KEPT_SLOTS // 8, 2)
    counts = jax.random.randint(count_key, (SEQUENCE_SHARDS,), lowest, KEPT_SLOTS + 1)
    full = jax.random.randint(full_key, (), 0, SEQUENCE_SHARDS)
    shard_ids = jnp.arange(SEQUENCE_SHARDS)
    counts = jnp.where(shard_ids == full, KEPT_SLOTS, counts)
    counts = jnp.where(shard_ids == (full + 1) % SEQUENCE_SHARDS, lowest, counts)
    shard_keys = jax.random.split(place_key, SEQUENCE_SHARDS)
    offsets = jax.vmap(lambda each: jnp.sort(jax.random.permutation(each, REGION)[:KEPT_SLOTS]))(shard_keys)
    slot_ids = jnp.arange(KEPT_SLOTS)
    first_zero = (shard_ids[:, None] == full) & (slot_ids[None, :] == 0)
    offsets = jnp.where(first_zero, 0, offsets)
    return jnp.where(slot_ids[None, :] < counts[:, None], offsets, REGION).astype(jnp.int32)


def level_of(key, extent, shards, low, top_value):
    def one(axis_at, parts):
        heights = jax.random.uniform(jax.random.fold_in(jax.random.fold_in(key, 6), axis_at), (parts,), jnp.float32, low / len(shards), top_value / len(shards))
        return jnp.repeat(jnp.exp(heights), extent[axis_at] // parts).reshape((-1,) + (1,) * (len(extent) - axis_at - 1))

    loudness = one(*shards[0])
    for cut in shards[1:]:
        loudness = loudness * one(*cut)
    return loudness


def centred(stream_key, extent, scale, bound, shards=(), held_as=jnp.bfloat16):
    gain = level_of(stream_key, extent, shards, -0.22, 0.18) if shards else 1.0
    array = jax.random.normal(stream_key, extent, jnp.float32) * scale * gain
    return jnp.minimum(jnp.maximum(array, -bound), bound).astype(held_as)


def setup_inputs(seed: int = 0) -> dict:
    splits = jax.random.split(jax.random.key(seed), 7)
    return {
        "queries": draw_queries(jax.random.fold_in(splits[6], 71), 0),
        "keys": draw_keys(jax.random.fold_in(splits[6], 71), 0),
        "values": centred(splits[2], (TOKEN_SLOTS, KEY_VALUE_HEADS, HEAD_SIZE), 1.0, 6.0, ((0, 256),)),
        "output_gradient": centred(splits[3], (TOKEN_SLOTS, QUERY_HEADS, HEAD_SIZE), 1.0, 6.0, ((0, 256),)),
        "kept_offset": draw_kept_offset(jax.random.fold_in(splits[6], 71), 0),
        "region_pos": jax.random.permutation(splits[5], SEQUENCE_SHARDS).astype(jnp.int32),
    }


def reference(queries, keys, values, output_gradient, kept_offset, region_pos):
    shard_list = N_OUTER * N_INNER
    context_group = QUERY_HEADS // KEY_VALUE_HEADS
    scale = HEAD_SIZE ** -0.5
    queries_full = queries.reshape(shard_list, KEPT_SLOTS, KEY_VALUE_HEADS, context_group, HEAD_SIZE)
    gradient_full = output_gradient.reshape(shard_list, KEPT_SLOTS, KEY_VALUE_HEADS, context_group, HEAD_SIZE)
    keys_full = keys.reshape(shard_list, KEPT_SLOTS, KEY_VALUE_HEADS, HEAD_SIZE)
    values_full = values.reshape(shard_list, KEPT_SLOTS, KEY_VALUE_HEADS, HEAD_SIZE)
    live_all = kept_offset < REGION
    positions = jnp.arange(KEPT_SLOTS, dtype=jnp.int32)
    causal = positions[None, :] <= positions[:, None]
    lanes = jnp.arange(N_INNER, dtype=jnp.int32)

    def one_shard(carry, device):
        key_running_sum, value_running_sum = carry
        outer_id = device // N_INNER
        window = jnp.concatenate([outer_id * N_INNER + lanes, ((outer_id - 1) % N_OUTER) * N_INNER + lanes]).astype(jnp.int32)
        query = queries_full[device].astype(jnp.float32)
        grad = gradient_full[device].astype(jnp.float32)
        key_win = keys_full[window].astype(jnp.float32)
        value_win = values_full[window].astype(jnp.float32)
        live_q = live_all[device]
        earlier = region_pos[window] < region_pos[device]
        same = window == device
        mask = live_q[:, None, None] & live_all[window][None, :, :] & (earlier[None, :, None] | (same[None, :, None] & causal[:, None, :]))
        scores = jnp.einsum("tgjc,eugc->gjteu", query, key_win) * scale
        masked = jnp.where(mask, scores, -jnp.inf)
        row_max = jnp.where(live_q, jnp.max(masked, axis=(3, 4)), 0.0)
        expo = jnp.where(mask, jnp.exp(scores - row_max[..., None, None]), 0.0)
        total = jnp.sum(expo, axis=(3, 4))
        safe = jnp.where(live_q, total, 1.0)
        weights = lax.optimization_barrier(expo.astype(jnp.bfloat16)).astype(jnp.float32)
        mixed = jnp.einsum("gjteu,eugc->gjtc", weights, value_win)
        result = jnp.where(live_q[:, None], mixed / safe[..., None], 0.0)
        out_low = result.transpose(2, 0, 1, 3).astype(jnp.bfloat16)
        log_norm = row_max + jnp.log(safe)
        delta = jnp.sum(grad * out_low.astype(jnp.float32), axis=-1).transpose(1, 2, 0)
        probs = jnp.where(mask, jnp.exp(scores - log_norm[..., None, None]), 0.0)
        probs_low = lax.optimization_barrier(probs.astype(jnp.bfloat16)).astype(jnp.float32)
        value_terms = jnp.einsum("gjteu,tgjc->eugc", probs_low, grad)
        grad_probs = jnp.einsum("tgjc,eugc->gjteu", grad, value_win)
        grad_scores = lax.optimization_barrier((probs * (grad_probs - delta[..., None, None])).astype(jnp.bfloat16)).astype(jnp.float32)
        grad_query = jnp.einsum("gjteu,eugc->tgjc", grad_scores, key_win) * scale
        key_terms = jnp.einsum("gjteu,tgjc->eugc", grad_scores, query) * scale
        key_terms = lax.optimization_barrier(key_terms.astype(jnp.bfloat16)).astype(jnp.float32)
        value_terms = lax.optimization_barrier(value_terms.astype(jnp.bfloat16)).astype(jnp.float32)
        key_running_sum = key_running_sum.at[window].add(key_terms)
        value_running_sum = value_running_sum.at[window].add(value_terms)
        return (key_running_sum, value_running_sum), (out_low, grad_query.astype(jnp.bfloat16))

    zero_array = jnp.zeros((shard_list, KEPT_SLOTS, KEY_VALUE_HEADS, HEAD_SIZE), jnp.float32)
    (key_running_sum, value_running_sum), (outs, grads) = lax.scan(one_shard, (zero_array, zero_array), jnp.arange(shard_list, dtype=jnp.int32))
    attn_out = outs.reshape(TOKEN_SLOTS, QUERY_HEADS, HEAD_SIZE)
    grad_queries = grads.reshape(TOKEN_SLOTS, QUERY_HEADS, HEAD_SIZE)
    key_gradient = key_running_sum.reshape(TOKEN_SLOTS, KEY_VALUE_HEADS, HEAD_SIZE).astype(jnp.bfloat16)
    value_gradient = value_running_sum.reshape(TOKEN_SLOTS, KEY_VALUE_HEADS, HEAD_SIZE).astype(jnp.bfloat16)
    return (attn_out, grad_queries, key_gradient, value_gradient)
```

```python
import functools
import math

import jax
import jax.numpy as jnp
from jax import lax
from jax.experimental import pallas as pl
from jax.experimental.pallas import tpu as pltpu
from jax.sharding import Mesh
from jax.sharding import PartitionSpec as P

REGION = 1024
SLOTS = 128
WIDTH = 128
HEADS_Q = 32
HEADS_KV = 4
N_OUTER = 16
N_Y = 2
N_X = 4
N_CORE = 2
WINDOW = 32
KEY_ROWS = WINDOW * SLOTS
PIECES = 8

QUERY_AXES = ("x", "core")
SHARDS = N_X * N_CORE
HEADS = HEADS_Q // SHARDS
QUERY_ROWS = SHARDS * SLOTS
TILES = SHARDS
LANES = HEADS * SLOTS
UNIT = 256
SPAN = 512
UNITS = KEY_ROWS // UNIT

FILL = -1e30
FLOOR = -1e29
SCALE = WIDTH ** (-0.5)
BASE_TWO = SCALE * math.log2(math.e)
BF16, F32, I32 = jnp.bfloat16, jnp.float32, jnp.int32

KEY_ORDER = 0
KEY_OFFSET = 32
KEY_COUNT = 64
QUERY_ORDER = 96
QUERY_OFFSET = 112
QUERY_COUNT = 128
QUERY_KEY = 144
REACH = 160
CLEAR = 176
TILE_COUNT = 192
SCALARS = 193


def slots():
    return lax.broadcasted_iota(I32, (SLOTS, WIDTH), 0)


def up(n, unit):
    return (n + unit - 1) // unit


def tile_rows(i):
    return pl.ds(pl.multiple_of(i * SLOTS, SLOTS), SLOTS)


def unit_rows(u, rows):
    return pl.ds(pl.multiple_of(u * UNIT, UNIT), rows)


def pack_rows(sc, array, packed):
    slot = slots()
    packed[:, tile_rows(sc[TILE_COUNT] - 1), :] = jnp.zeros((HEADS, SLOTS, WIDTH), F32)

    @pl.loop(0, SHARDS)
    def _(j):
        s = sc[QUERY_ORDER + j]
        live = (slot < sc[QUERY_COUNT + s])[None]
        packed[:, pl.ds(sc[QUERY_OFFSET + s], SLOTS), :] = jnp.where(live, array[s].astype(F32), 0.0)


def unpack_rows(sc, packed, array):
    slot = slots()

    @pl.loop(0, SHARDS)
    def _(s):
        live = (slot < sc[QUERY_COUNT + s])[None]
        rows = packed[:, pl.ds(sc[QUERY_OFFSET + s], SLOTS), :]
        array[s] = jnp.where(live, rows, 0.0).astype(BF16)


def shown(s, unit, limit):
    place = lax.broadcasted_iota(I32, s.shape, 0)
    return jnp.where(place <= limit - unit * UNIT, s, FILL)


def over_keys(sc, i, step, carry):
    clear = sc[CLEAR + i]
    carry = lax.fori_loop(
        0, clear, lambda n, c: step(n * (SPAN // UNIT), SPAN // UNIT, False, c), carry
    )
    return lax.fori_loop(
        clear * (SPAN // UNIT), up(sc[REACH + i], UNIT), lambda u, c: step(u, 1, True, c), carry
    )


def fold(op, s):
    return op(s.reshape(-1, 8, s.shape[1]), axis=0)


def turned(ref, u, units):
    return jnp.concatenate([ref[u + n] for n in range(units)], axis=1)


def forward(sc, q_ref, *refs):
    pieces, rest = refs[:PIECES], refs[PIECES:]
    o_ref, oc, qc, kc, vc, kt, norm_ref, limit_ref, stage, kf, vf, vt, qf, of, thr, scr = rest
    slot = slots()
    tiles = sc[TILE_COUNT]
    most = sc[REACH + tiles - 1]
    for p, ref in enumerate(pieces):
        stage[p * N_X : (p + 1) * N_X] = ref[...]
    tail = unit_rows(up(most, UNIT) - 1, UNIT)
    kf[tail, :] = jnp.zeros((UNIT, WIDTH), F32)
    vf[tail, :] = jnp.zeros((UNIT, WIDTH), F32)

    @pl.loop(0, WINDOW)
    def _(j):
        w = sc[KEY_ORDER + j]
        rows = pl.ds(sc[KEY_OFFSET + w], SLOTS)
        kf[rows, :] = stage[w, 0].astype(F32)
        vf[rows, :] = stage[w, 1].astype(F32)

    @pl.loop(0, up(most, UNIT))
    def _(u):
        rows = unit_rows(u, UNIT)
        keys = kf[rows, :].astype(BF16)
        vals = vf[rows, :].astype(BF16)
        kc[rows, :] = keys
        vc[rows, :] = vals
        kt[u] = keys.T
        vt[u] = vals.T

    thr[tile_rows(tiles - 1), :] = jnp.full((SLOTS, WIDTH), -1, I32)

    @pl.loop(0, SHARDS)
    def _(j):
        s = sc[QUERY_ORDER + j]
        thr[pl.ds(sc[QUERY_OFFSET + s], SLOTS), :] = jnp.where(
            slot < sc[QUERY_COUNT + s], slot + sc[QUERY_KEY + s], -1
        )

    pack_rows(sc, q_ref, qf)

    @pl.loop(0, tiles)
    def _(i):
        rows = tile_rows(i)
        limit = jnp.concatenate([thr[rows, :].T[0:1, :]] * HEADS, axis=1)
        limit_ref[i] = limit
        q_tile = qf[:, rows, :].astype(BF16)
        qc[:, rows, :] = q_tile
        q_turn = q_tile.reshape(LANES, WIDTH).T

        def score(u, units, masked, top):
            s = jnp.dot(kc[unit_rows(u, units * UNIT), :], q_turn, preferred_element_type=F32)
            if masked:
                s = shown(s, u, limit)
            scr[unit_rows(u, units * UNIT), :] = s
            return jnp.maximum(top, fold(jnp.max, s))

        top = over_keys(sc, i, score, jnp.full((8, LANES), FLOOR, F32))
        top = jnp.max(top, axis=0, keepdims=True) * BASE_TWO

        def weigh(u, units, masked, carry):
            total, acc = carry
            w = jnp.exp2(scr[unit_rows(u, units * UNIT), :] * BASE_TWO - top)
            total = total + fold(jnp.sum, w)
            acc = acc + jnp.dot(turned(vt, u, units), w.astype(BF16), preferred_element_type=F32)
            return total, acc

        total, acc = over_keys(
            sc, i, weigh, (jnp.zeros((8, LANES), F32), jnp.zeros((WIDTH, LANES), F32))
        )
        total = jnp.sum(total, axis=0, keepdims=True)
        total = jnp.where(total > 0.0, total, 1.0)
        norm_ref[i] = top + jnp.log2(total)
        out = (acc * (1.0 / total)).T.reshape(HEADS, SLOTS, WIDTH)
        of[:, rows, :] = out
        oc[:, rows, :] = out.astype(BF16)

    unpack_rows(sc, of, o_ref)


def backward(sc, g_ref, oc, qc, kc, vc, kt, norm_ref, limit_ref, dq_ref, near_ref, far_ref, gf, dqf, dk, dv):
    @pl.loop(0, UNITS)
    def _(u):
        dk[unit_rows(u, UNIT), :] = jnp.zeros((UNIT, WIDTH), F32)
        dv[unit_rows(u, UNIT), :] = jnp.zeros((UNIT, WIDTH), F32)

    pack_rows(sc, g_ref, gf)

    @pl.loop(0, sc[TILE_COUNT])
    def _(i):
        rows = tile_rows(i)
        limit = limit_ref[i]
        norm = norm_ref[i]
        q_tile = qc[:, rows, :].reshape(LANES, WIDTH)
        g_tile = gf[:, rows, :].astype(BF16).reshape(LANES, WIDTH)
        q_turn = q_tile.T
        g_turn = g_tile.T
        o_turn = oc[:, rows, :].reshape(LANES, WIDTH).T
        delta = jnp.sum(g_turn.astype(F32) * o_turn.astype(F32), axis=0, keepdims=True)

        def step(u, units, masked, acc):
            at = unit_rows(u, units * UNIT)
            s = jnp.dot(kc[at, :], q_turn, preferred_element_type=F32)
            dp = jnp.dot(vc[at, :], g_turn, preferred_element_type=F32)
            if masked:
                s = shown(s, u, limit)
            p = jnp.exp2(s * BASE_TWO - norm)
            ds = (p * (dp - delta)).astype(BF16)
            dv[at, :] += jnp.dot(p.astype(BF16), g_tile, preferred_element_type=F32)
            dk[at, :] += jnp.dot(ds, q_tile, preferred_element_type=F32)
            return acc + jnp.dot(turned(kt, u, units), ds, preferred_element_type=F32)

        acc = over_keys(sc, i, step, jnp.zeros((WIDTH, LANES), F32))
        dqf[:, rows, :] = (acc * SCALE).T.reshape(HEADS, SLOTS, WIDTH)

    unpack_rows(sc, dqf, dq_ref)
    slot = slots()
    for g in range(2):
        for far in range(2):
            ref = far_ref if far else near_ref

            @pl.loop(0, 2 * N_X)
            def _(e, g=g, far=far, ref=ref):
                y, x = e // N_X, e % N_X
                w = g * 16 + far * 8 + e
                rows = pl.ds(sc[KEY_OFFSET + w], SLOTS)
                live = slot < sc[KEY_COUNT + w]
                ref[g, y, x, 0] = jnp.where(live, dk[rows, :] * SCALE, 0.0).astype(BF16)
                ref[g, y, x, 1] = jnp.where(live, dv[rows, :], 0.0).astype(BF16)


ROWS = (SHARDS, HEADS, SLOTS, WIDTH)
PACKED_ROWS = (HEADS, QUERY_ROWS, WIDTH)
PACKING_ROWS = pltpu.VMEM((HEADS, QUERY_ROWS + SLOTS, WIDTH), F32)
PACKING_KEYS = pltpu.VMEM((KEY_ROWS + SLOTS, WIDTH), F32)


def call(kernel, operands, out_shape, scratch, matmuls, name):
    vmem = pl.BlockSpec(memory_space=pltpu.VMEM)
    pairs = LANES * QUERY_ROWS // SLOTS * KEY_ROWS // 6
    return pl.pallas_call(
        kernel,
        out_shape=out_shape,
        in_specs=[pl.BlockSpec(memory_space=pltpu.SMEM)] + [vmem] * (len(operands) - 1),
        out_specs=(vmem,) * len(out_shape),
        scratch_shapes=scratch,
        compiler_params=pltpu.CompilerParams(vmem_limit_bytes=56 * 1024 * 1024),
        cost_estimate=pl.CostEstimate(
            flops=matmuls * 2 * pairs * WIDTH, bytes_accessed=8 << 20, transcendentals=pairs
        ),
        name=name,
    )(*operands)


def run_forward(scalars, q, pieces):
    shape = jax.ShapeDtypeStruct
    turned_keys = (UNITS, WIDTH, UNIT)
    o, *packed = call(
        forward,
        (scalars, q, *pieces),
        (
            shape(ROWS, BF16),
            shape(PACKED_ROWS, BF16),
            shape(PACKED_ROWS, BF16),
            shape((KEY_ROWS, WIDTH), BF16),
            shape((KEY_ROWS, WIDTH), BF16),
            shape(turned_keys, BF16),
            shape((TILES, 1, LANES), F32),
            shape((TILES, 1, LANES), I32),
        ),
        [
            pltpu.VMEM((WINDOW, 2, SLOTS, WIDTH), BF16),
            PACKING_KEYS,
            PACKING_KEYS,
            pltpu.VMEM(turned_keys, BF16),
            PACKING_ROWS,
            PACKING_ROWS,
            pltpu.VMEM((QUERY_ROWS + SLOTS, WIDTH), I32),
            pltpu.VMEM((KEY_ROWS, LANES), F32),
        ],
        2,
        "window_forward",
    )
    return o, packed


def run_backward(scalars, g, packed):
    terms = jax.ShapeDtypeStruct((2, 2, N_X, 2, SLOTS, WIDTH), BF16)
    return call(
        backward,
        (scalars, g, *packed),
        (jax.ShapeDtypeStruct(ROWS, BF16), terms, terms),
        [PACKING_ROWS, PACKING_ROWS, PACKING_KEYS, PACKING_KEYS],
        5,
        "window_backward",
    )


def plan(kept_offset, region_pos):
    outer, y, x_, core = (lax.axis_index(a) for a in ("outer", "y", "x", "core"))
    shard = jnp.arange(N_OUTER * N_Y * N_X * N_CORE)
    counts = jnp.sum((kept_offset < REGION).astype(jnp.int32), axis=1)

    def pick(ids):
        hit = ids[:, None] == shard[None, :]
        of = lambda a: jnp.sum(jnp.where(hit, a[None, :], 0), axis=1)
        return of(counts), of(region_pos)

    w = jnp.arange(WINDOW)
    g, p, x = w // 16, w // 4 % 4, (x_ - w) % 4
    group = jnp.where(g == 0, outer, (outer - 1) % N_OUTER)
    count, place = pick(
        group * 16 + ((y ^ (p % 2)) * N_X + x) * N_CORE + (core ^ (p // 2))
    )
    before = place[None, :] < place[:, None]
    offset = jnp.sum(jnp.where(before, count[None, :], 0), axis=1)
    rank = jnp.sum(before.astype(jnp.int32), axis=1)
    order = jnp.sum(jnp.where(rank[None, :] == w[:, None], w[None, :], 0), axis=1)

    s = jnp.arange(SHARDS)
    q_count, q_place = pick(outer * 16 + (y * N_X + s // 2) * N_CORE + s % 2)
    q_before = q_place[None, :] < q_place[:, None]
    q_offset = jnp.sum(jnp.where(q_before, q_count[None, :], 0), axis=1)
    q_rank = jnp.sum(q_before.astype(jnp.int32), axis=1)
    q_order = jnp.sum(jnp.where(q_rank[None, :] == s[:, None], s[None, :], 0), axis=1)
    q_key = jnp.sum(jnp.where(place[None, :] < q_place[:, None], count[None, :], 0), axis=1)

    start = jnp.arange(TILES)[:, None] * SLOTS
    within = (q_offset[None, :] < start + SLOTS) & (q_offset[None, :] + q_count[None, :] > start)
    end = q_key[None, :] + jnp.minimum(q_count[None, :], start + SLOTS - q_offset[None, :])
    reach = jnp.max(jnp.where(within, end, 0), axis=1)
    first = q_key[None, :] + jnp.maximum(start - q_offset[None, :], 0)
    clear = (jnp.min(jnp.where(within, first, KEY_ROWS), axis=1) + 1) // SPAN
    tiles = (jnp.sum(q_count) + SLOTS - 1) // SLOTS

    pad = lambda a, n: jnp.pad(a, (0, n - a.shape[0]))
    return jnp.concatenate([
        order, offset, count,
        pad(q_order, 16), pad(q_offset, 16), pad(q_count, 16), pad(q_key, 16), pad(reach, 16),
        pad(clear, 16),
        tiles[None],
    ]).astype(jnp.int32)


def total(*parts):
    return functools.reduce(jnp.add, [a.astype(F32) for a in parts]).astype(BF16)


def to_x(block, step):
    return lax.ppermute(block, "x", [(i, (i + step) % N_X) for i in range(N_X)])


def to_core(block):
    return lax.ppermute(block, "core", [(0, 1), (1, 0)])


def to_group(block, step, flip):
    route = [
        (i * 2 + y, (i + step) % N_OUTER * 2 + (y ^ flip))
        for i in range(N_OUTER)
        for y in range(N_Y)
    ]
    return lax.ppermute(block, ("outer", "y"), route)


def on_device(queries, keys, values, output_gradient, kept_offset, region_pos):
    x = lax.axis_index("x")
    exchange = functools.partial(lax.all_to_all, split_axis=0, concat_axis=0, tiled=True)
    scalars = plan(kept_offset, region_pos)

    kv = jnp.stack([keys, values]).transpose(2, 0, 1, 3)
    kv = [lax.dynamic_index_in_dim(kv, (x + k) % N_X, 0, keepdims=False) for k in range(N_X)]
    own = jnp.stack([to_x(kv[k], k) if k else kv[0] for k in range(N_X)])
    turned_queries, own = lax.optimization_barrier((queries.transpose(1, 0, 2), own))
    own_pair = (own, to_group(own, 0, 1))
    prev_pair = (to_group(own, 1, 0), to_group(own, 1, 1))
    pieces = (
        *own_pair, *(to_core(a) for a in own_pair), *prev_pair, *(to_core(a) for a in prev_pair)
    )

    q = exchange(turned_queries, QUERY_AXES).reshape(ROWS)
    gradient, q = lax.optimization_barrier((output_gradient.transpose(1, 0, 2), q))
    g = exchange(gradient, QUERY_AXES).reshape(ROWS)

    o, packed = run_forward(scalars, q, pieces)
    o_home = exchange(o.reshape(HEADS_Q, SLOTS, WIDTH), QUERY_AXES)
    dq, near, far = run_backward(scalars, g, packed)

    o_home, dq, near, far = lax.optimization_barrier((o_home, dq, near, far))
    far = to_core(far)
    term = lambda g, y: total(near[g, y], far[g, y])
    sums = total(
        term(0, 0),
        to_group(term(0, 1), 0, 1),
        to_group(term(1, 0), -1, 0),
        to_group(term(1, 1), -1, 1),
    )
    grads = [to_x(sums[k], -k) if k else sums[0] for k in range(N_X)]
    grads = jnp.stack([lax.select_n((h - x) % N_X, *grads) for h in range(N_X)])
    dq_home = exchange(dq.reshape(HEADS_Q, SLOTS, WIDTH), QUERY_AXES)

    return (
        o_home.transpose(1, 0, 2),
        dq_home.transpose(1, 0, 2),
        grads[:, 0].transpose(1, 0, 2),
        grads[:, 1].transpose(1, 0, 2),
    )


def solution(mesh):
    devices = mesh.devices.reshape(N_OUTER, N_Y, N_X, N_CORE)
    split = Mesh(devices, ("outer", "y", "x", "core"))
    rows = P(("outer", "y", "x", "core"), None, None)
    return jax.shard_map(
        on_device,
        mesh=split,
        in_specs=(rows, rows, rows, rows, P(), P()),
        out_specs=(rows, rows, rows, rows),
        check_vma=False,
    )
```

```python
import functools
import math

import jax
import jax.numpy as jnp
from jax import lax
from jax.experimental import pallas as pl
from jax.experimental.pallas import tpu as pltpu
from jax.sharding import Mesh
from jax.sharding import PartitionSpec as P

REGION = 1024
SLOTS = 128
WIDTH = 128
HEADS_Q = 32
HEADS_KV = 4
N_OUTER = 16
N_Y = 2
N_X = 4
N_CORE = 2
WINDOW = 32
KEY_ROWS = WINDOW * SLOTS
PIECES = 8

QUERY_AXES = ("x", "core")
SHARDS = N_X * N_CORE
HEADS = HEADS_Q // SHARDS
QUERY_ROWS = SHARDS * SLOTS
TILES = SHARDS
LANES = HEADS * SLOTS
UNIT = 256
SPAN = 512
UNITS = KEY_ROWS // UNIT
SAFE = 60.0

FILL = -1e30
FLOOR = -1e29
SCALE = WIDTH ** (-0.5)
BASE_TWO = SCALE * math.log2(math.e)
BF16, F32, I32 = jnp.bfloat16, jnp.float32, jnp.int32

KEY_ORDER = 0
KEY_OFFSET = 32
KEY_COUNT = 64
QUERY_ORDER = 96
QUERY_OFFSET = 112
QUERY_COUNT = 128
QUERY_KEY = 144
REACH = 160
TILE_COUNT = 176


def slots():
    return lax.broadcasted_iota(I32, (SLOTS, WIDTH), 0)


def up(n, unit):
    return (n + unit - 1) // unit


def tile_rows(i):
    return pl.ds(pl.multiple_of(i * SLOTS, SLOTS), SLOTS)


def unit_rows(u, rows):
    return pl.ds(pl.multiple_of(u * UNIT, UNIT), rows)


def pack_rows(sc, array, part, packed):
    slot = slots()
    packed[:, tile_rows(sc[TILE_COUNT] - 1), :] = jnp.zeros((HEADS, SLOTS, WIDTH), F32)

    @pl.loop(0, SHARDS)
    def _(j):
        s = sc[QUERY_ORDER + j]
        live = (slot < sc[QUERY_COUNT + s])[None]
        packed[:, pl.ds(sc[QUERY_OFFSET + s], SLOTS), :] = jnp.where(
            live, array[s, part].astype(F32), 0.0
        )


def unpack_rows(sc, packed, array, part):
    slot = slots()

    @pl.loop(0, SHARDS)
    def _(s):
        live = (slot < sc[QUERY_COUNT + s])[None]
        rows = packed[:, pl.ds(sc[QUERY_OFFSET + s], SLOTS), :]
        array[s, part] = jnp.where(live, rows, 0.0).astype(BF16)


def shown(s, first, limit):
    place = lax.broadcasted_iota(I32, s.shape, 0)
    return jnp.where(place <= limit - first, s, FILL)


def fold(op, s):
    return op(s.reshape(-1, 8, s.shape[1]), axis=0)


def square(a):
    a = a.astype(F32)
    return jnp.sum(a * a, axis=0, keepdims=True)


def attend(sc, rows_ref, *refs):
    pieces, (out_ref, near_ref, far_ref), scratch = refs[:PIECES], refs[PIECES : PIECES + 3], refs[PIECES + 3 :]
    stage, raw, kf, vf, kc, vc, kt, vt, qf, gf, of, dqf, thr, wb, db, dk, dv, sems = scratch
    slot = slots()
    tiles = sc[TILE_COUNT]
    spans = up(sc[REACH + tiles - 1], SPAN)

    copies = [
        pltpu.make_async_copy(ref, stage.at[pl.ds(p * N_X, N_X)], sems.at[p])
        for p, ref in enumerate(pieces)
    ]
    rows_copy = pltpu.make_async_copy(rows_ref, raw, sems.at[PIECES])
    for copy in copies:
        copy.start()
    rows_copy.start()

    tail = pl.ds(pl.multiple_of((spans - 1) * SPAN, SPAN), SPAN)
    kf[tail, :] = jnp.zeros((SPAN, WIDTH), F32)
    vf[tail, :] = jnp.zeros((SPAN, WIDTH), F32)
    thr[tile_rows(tiles - 1), :] = jnp.full((SLOTS, WIDTH), -1, I32)

    @pl.loop(0, UNITS)
    def _(u):
        dk[unit_rows(u, UNIT), :] = jnp.zeros((UNIT, WIDTH), F32)
        dv[unit_rows(u, UNIT), :] = jnp.zeros((UNIT, WIDTH), F32)

    @pl.loop(0, SHARDS)
    def _(j):
        s = sc[QUERY_ORDER + j]
        thr[pl.ds(sc[QUERY_OFFSET + s], SLOTS), :] = jnp.where(
            slot < sc[QUERY_COUNT + s], slot + sc[QUERY_KEY + s], -1
        )

    for copy in copies:
        copy.wait()

    @pl.loop(0, WINDOW)
    def _(j):
        w = sc[KEY_ORDER + j]
        rows = pl.ds(sc[KEY_OFFSET + w], SLOTS)
        kf[rows, :] = stage[w, 0].astype(F32)
        vf[rows, :] = stage[w, 1].astype(F32)

    def turn(u, longest):
        rows = unit_rows(u, UNIT)
        keys = kf[rows, :].astype(BF16)
        vals = vf[rows, :].astype(BF16)
        kc[rows, :] = keys
        vc[rows, :] = vals
        keys = keys.T
        kt[u] = keys
        vt[u] = vals.T
        return jnp.maximum(longest, square(keys))

    longest = lax.fori_loop(0, spans * (SPAN // UNIT), turn, jnp.zeros((1, UNIT), F32))
    longest = jnp.max(longest)

    rows_copy.wait()
    pack_rows(sc, raw, 0, qf)
    pack_rows(sc, raw, 1, gf)

    @pl.loop(0, tiles)
    def _(i):
        rows = tile_rows(i)
        count = up(sc[REACH + i], SPAN)
        units = up(sc[REACH + i], UNIT)
        limit = jnp.concatenate([thr[rows, :].T[0:1, :]] * HEADS, axis=1)
        q_tile = qf[:, rows, :].astype(BF16).reshape(LANES, WIDTH)
        q_turn = q_tile.T
        safe = jnp.max(square(q_turn)) * longest * BASE_TWO ** 2 <= SAFE ** 2

        def span_rows(n):
            return pl.ds(pl.multiple_of(n * SPAN, SPAN), SPAN)

        def scores(n):
            s = jnp.dot(kc[span_rows(n), :], q_turn, preferred_element_type=F32)
            return shown(s, n * SPAN, limit)

        top = lax.fori_loop(
            0,
            jnp.where(safe, 0, count),
            lambda n, top: jnp.maximum(top, fold(jnp.max, scores(n))),
            jnp.full((8, LANES), jnp.where(safe, 0.0, FLOOR), F32),
        )
        top = jnp.max(top, axis=0, keepdims=True) * BASE_TWO

        def weigh(n):
            w = jnp.exp2(scores(n) * BASE_TWO - top)
            wb[span_rows(n), :] = w.astype(BF16)
            return fold(jnp.sum, w)

        def mix(n):
            vals = jnp.concatenate(
                [vt[n * (SPAN // UNIT) + m] for m in range(SPAN // UNIT)], axis=1
            )
            return jnp.dot(vals, wb[span_rows(n), :], preferred_element_type=F32)

        def step(n, carry):
            total, acc = carry
            acc = acc + mix(n - 1)
            return total + weigh(n), acc

        total = weigh(0)
        total, acc = lax.fori_loop(1, count, step, (total, jnp.zeros((WIDTH, LANES), F32)))
        acc = acc + mix(count - 1)
        total = jnp.sum(total, axis=0, keepdims=True)
        inverse = 1.0 / jnp.where(total > 0.0, total, 1.0)
        out = (acc * inverse).astype(BF16)
        of[:, rows, :] = out.T.astype(F32).reshape(HEADS, SLOTS, WIDTH)

        g_turn = gf[:, rows, :].astype(BF16).reshape(LANES, WIDTH).T.astype(F32) * inverse
        g_turn = g_turn.astype(BF16)
        delta = jnp.sum(g_turn.astype(F32) * out.astype(F32), axis=0, keepdims=True)
        g_tile = g_turn.T

        def weigh_back(u):
            at = unit_rows(u, UNIT)
            dp = jnp.dot(vc[at, :], g_turn, preferred_element_type=F32)
            db[...] = (wb[at, :].astype(F32) * (dp - delta)).astype(BF16)

        def mix_back(u, acc):
            at = unit_rows(u, UNIT)
            dv[at, :] += jnp.dot(wb[at, :], g_tile, preferred_element_type=F32)
            dk[at, :] += jnp.dot(db[...], q_tile, preferred_element_type=F32)
            return acc + jnp.dot(kt[u], db[...], preferred_element_type=F32)

        def step_back(u, acc):
            acc = mix_back(u - 1, acc)
            weigh_back(u)
            return acc

        weigh_back(0)
        acc = lax.fori_loop(1, units, step_back, jnp.zeros((WIDTH, LANES), F32))
        acc = mix_back(units - 1, acc)
        dqf[:, rows, :] = (acc * SCALE).astype(BF16).T.astype(F32).reshape(HEADS, SLOTS, WIDTH)

    unpack_rows(sc, of, out_ref, 0)
    unpack_rows(sc, dqf, out_ref, 1)
    for g in range(2):
        for far in range(2):
            ref = far_ref if far else near_ref

            @pl.loop(0, 2 * N_X)
            def _(e, g=g, far=far, ref=ref):
                y, x = e // N_X, e % N_X
                w = g * 16 + far * 8 + e
                rows = pl.ds(sc[KEY_OFFSET + w], SLOTS)
                live = slot < sc[KEY_COUNT + w]
                ref[g, y, x, 0] = jnp.where(live, dk[rows, :] * SCALE, 0.0).astype(BF16)
                ref[g, y, x, 1] = jnp.where(live, dv[rows, :], 0.0).astype(BF16)


ROWS = (SHARDS, 2, HEADS, SLOTS, WIDTH)


def attention(scalars, rows, pieces):
    terms = jax.ShapeDtypeStruct((2, 2, N_X, 2, SLOTS, WIDTH), BF16)
    any_place = pl.BlockSpec(memory_space=pl.ANY)
    vmem = pl.BlockSpec(memory_space=pltpu.VMEM)
    packing_keys = pltpu.VMEM((KEY_ROWS + SLOTS, WIDTH), F32)
    packing_rows = pltpu.VMEM((HEADS, QUERY_ROWS + SLOTS, WIDTH), F32)
    keys = pltpu.VMEM((KEY_ROWS, WIDTH), BF16)
    turned_keys = pltpu.VMEM((UNITS, WIDTH, UNIT), BF16)
    return pl.pallas_call(
        attend,
        out_shape=(jax.ShapeDtypeStruct(ROWS, BF16), terms, terms),
        in_specs=[pl.BlockSpec(memory_space=pltpu.SMEM)] + [any_place] * (1 + PIECES),
        out_specs=(vmem,) * 3,
        scratch_shapes=[
            pltpu.VMEM((WINDOW, 2, SLOTS, WIDTH), BF16),
            pltpu.VMEM(ROWS, BF16),
            *[packing_keys] * 2,
            *[keys] * 2,
            *[turned_keys] * 2,
            *[packing_rows] * 4,
            pltpu.VMEM((QUERY_ROWS + SLOTS, WIDTH), I32),
            pltpu.VMEM((KEY_ROWS, LANES), BF16),
            pltpu.VMEM((UNIT, LANES), BF16),
            *[packing_keys] * 2,
            pltpu.SemaphoreType.DMA((PIECES + 1,)),
        ],
        compiler_params=pltpu.CompilerParams(vmem_limit_bytes=44 * 1024 * 1024),
        name="window_attention",
    )(scalars, rows, *pieces)


def plan(kept_offset, region_pos):
    outer, y, x_, core = (lax.axis_index(a) for a in ("outer", "y", "x", "core"))
    shard = jnp.arange(N_OUTER * N_Y * N_X * N_CORE)
    counts = jnp.sum((kept_offset < REGION).astype(jnp.int32), axis=1)

    def pick(ids):
        hit = ids[:, None] == shard[None, :]
        of = lambda a: jnp.sum(jnp.where(hit, a[None, :], 0), axis=1)
        return of(counts), of(region_pos)

    w = jnp.arange(WINDOW)
    g, p, x = w // 16, w // 4 % 4, (x_ - w) % 4
    group = jnp.where(g == 0, outer, (outer - 1) % N_OUTER)
    count, place = pick(
        group * 16 + ((y ^ (p % 2)) * N_X + x) * N_CORE + (core ^ (p // 2))
    )
    before = place[None, :] < place[:, None]
    offset = jnp.sum(jnp.where(before, count[None, :], 0), axis=1)
    rank = jnp.sum(before.astype(jnp.int32), axis=1)
    order = jnp.sum(jnp.where(rank[None, :] == w[:, None], w[None, :], 0), axis=1)

    s = jnp.arange(SHARDS)
    q_count, q_place = pick(outer * 16 + (y * N_X + s // 2) * N_CORE + s % 2)
    q_before = q_place[None, :] < q_place[:, None]
    q_offset = jnp.sum(jnp.where(q_before, q_count[None, :], 0), axis=1)
    q_rank = jnp.sum(q_before.astype(jnp.int32), axis=1)
    q_order = jnp.sum(jnp.where(q_rank[None, :] == s[:, None], s[None, :], 0), axis=1)
    q_key = jnp.sum(jnp.where(place[None, :] < q_place[:, None], count[None, :], 0), axis=1)

    start = jnp.arange(TILES)[:, None] * SLOTS
    within = (q_offset[None, :] < start + SLOTS) & (q_offset[None, :] + q_count[None, :] > start)
    end = q_key[None, :] + jnp.minimum(q_count[None, :], start + SLOTS - q_offset[None, :])
    reach = jnp.max(jnp.where(within, end, 0), axis=1)
    tiles = (jnp.sum(q_count) + SLOTS - 1) // SLOTS

    pad = lambda a, n: jnp.pad(a, (0, n - a.shape[0]))
    return jnp.concatenate([
        order, offset, count,
        pad(q_order, 16), pad(q_offset, 16), pad(q_count, 16), pad(q_key, 16), pad(reach, 16),
        tiles[None],
    ]).astype(jnp.int32)


def total(*parts):
    return functools.reduce(jnp.add, [a.astype(F32) for a in parts]).astype(BF16)


def to_x(block, step):
    return lax.ppermute(block, "x", [(i, (i + step) % N_X) for i in range(N_X)])


def to_core(block):
    return lax.ppermute(block, "core", [(0, 1), (1, 0)])


def to_group(block, step, flip):
    route = [
        (i * 2 + y, (i + step) % N_OUTER * 2 + (y ^ flip))
        for i in range(N_OUTER)
        for y in range(N_Y)
    ]
    return lax.ppermute(block, ("outer", "y"), route)


def on_device(queries, keys, values, output_gradient, kept_offset, region_pos):
    x = lax.axis_index("x")
    exchange = functools.partial(lax.all_to_all, split_axis=0, concat_axis=0, tiled=True)
    kv = jnp.stack([keys, values]).transpose(2, 0, 1, 3)
    kv = [lax.dynamic_index_in_dim(kv, (x + k) % N_X, 0, keepdims=False) for k in range(N_X)]
    own = jnp.stack([to_x(kv[k], k) if k else kv[0] for k in range(N_X)])

    def by_head(a):
        return a.transpose(1, 0, 2).reshape(SHARDS, HEADS, SLOTS, WIDTH)

    rows = jnp.stack([by_head(queries), by_head(output_gradient)], axis=1)
    own, rows, kept_offset, region_pos = lax.optimization_barrier(
        (own, rows, kept_offset, region_pos)
    )
    scalars = plan(kept_offset, region_pos)
    own_pair = (own, to_group(own, 0, 1))
    prev_pair = (to_group(own, 1, 0), to_group(own, 1, 1))
    pieces = (
        *own_pair, *(to_core(a) for a in own_pair), *prev_pair, *(to_core(a) for a in prev_pair)
    )

    rows = exchange(rows, QUERY_AXES)
    rows, near, far = attention(scalars, rows, pieces)
    far = to_core(far)
    term = lambda g, y: total(near[g, y], far[g, y])
    sums = total(
        term(0, 0),
        to_group(term(0, 1), 0, 1),
        to_group(term(1, 0), -1, 0),
        to_group(term(1, 1), -1, 1),
    )
    grads = [to_x(sums[k], -k) if k else sums[0] for k in range(N_X)]
    grads = jnp.stack([lax.select_n((h - x) % N_X, *grads) for h in range(N_X)])
    home = exchange(rows, QUERY_AXES)

    def by_slot(a):
        return a.reshape(HEADS_Q, SLOTS, WIDTH).transpose(1, 0, 2)

    return (
        by_slot(home[:, 0]),
        by_slot(home[:, 1]),
        grads[:, 0].transpose(1, 0, 2),
        grads[:, 1].transpose(1, 0, 2),
    )


def solution(mesh):
    devices = mesh.devices.reshape(N_OUTER, N_Y, N_X, N_CORE)
    split = Mesh(devices, ("outer", "y", "x", "core"))
    rows = P(("outer", "y", "x", "core"), None, None)
    return jax.shard_map(
        on_device,
        mesh=split,
        in_specs=(rows, rows, rows, rows, P(), P()),
        out_specs=(rows, rows, rows, rows),
        check_vma=False,
    )
```

```python
import functools
import math

import jax
import jax.numpy as jnp
from jax import lax
from jax.experimental import pallas as pl
from jax.experimental.pallas import tpu as pltpu
from jax.sharding import Mesh
from jax.sharding import PartitionSpec as P

REGION = 1024
SLOTS = 128
WIDTH = 128
HEADS_Q = 32
HEADS_KV = 4
N_OUTER = 16
N_Y = 2
N_X = 4
N_CORE = 2
WINDOW = 32
KEY_ROWS = WINDOW * SLOTS
PIECES = 8

QUERY_AXES = ("x", "core")
SHARDS = N_X * N_CORE
HEADS = HEADS_Q // SHARDS
QUERY_ROWS = SHARDS * SLOTS
TILES = SHARDS
LANES = HEADS * SLOTS
UNIT = 256
SPAN = 512
UNITS = KEY_ROWS // UNIT
SAFE = 60.0

FILL = -1e30
FLOOR = -1e29
SCALE = WIDTH ** (-0.5)
BASE_TWO = SCALE * math.log2(math.e)
BF16, F32, I32 = jnp.bfloat16, jnp.float32, jnp.int32

KEY_ORDER = 0
KEY_OFFSET = 32
KEY_COUNT = 64
QUERY_ORDER = 96
QUERY_OFFSET = 112
QUERY_COUNT = 128
QUERY_KEY = 144
REACH = 160
TILE_COUNT = 176


def slots():
    return lax.broadcasted_iota(I32, (SLOTS, WIDTH), 0)


def up(n, unit):
    return (n + unit - 1) // unit


def tile_rows(i):
    return pl.ds(pl.multiple_of(i * SLOTS, SLOTS), SLOTS)


def unit_rows(u, rows):
    return pl.ds(pl.multiple_of(u * UNIT, UNIT), rows)


def pack_rows(sc, array, part, packed):
    slot = slots()
    packed[:, tile_rows(sc[TILE_COUNT] - 1), :] = jnp.zeros((HEADS, SLOTS, WIDTH), F32)

    @pl.loop(0, SHARDS)
    def _(j):
        s = sc[QUERY_ORDER + j]
        live = (slot < sc[QUERY_COUNT + s])[None]
        packed[:, pl.ds(sc[QUERY_OFFSET + s], SLOTS), :] = jnp.where(
            live, array[s, part].astype(F32), 0.0
        )


def unpack_rows(sc, packed, array, part):
    slot = slots()

    @pl.loop(0, SHARDS)
    def _(s):
        live = (slot < sc[QUERY_COUNT + s])[None]
        rows = packed[:, pl.ds(sc[QUERY_OFFSET + s], SLOTS), :]
        array[s, part] = jnp.where(live, rows, 0.0).astype(BF16)


def shown(s, first, limit):
    place = lax.broadcasted_iota(I32, s.shape, 0)
    return jnp.where(place <= limit - first, s, FILL)


def fold(op, s):
    return op(s.reshape(-1, 8, s.shape[1]), axis=0)


def square(a):
    a = a.astype(F32)
    return jnp.sum(a * a, axis=0, keepdims=True)


def prepare(sc, *refs):
    pieces, (kc, vc, kt, vt, long_ref, stage, kf, vf, sems) = refs[:PIECES], refs[PIECES:]
    spans = up(sc[REACH + sc[TILE_COUNT] - 1], SPAN)
    copies = [
        pltpu.make_async_copy(ref, stage.at[pl.ds(p * N_X, N_X)], sems.at[p])
        for p, ref in enumerate(pieces)
    ]
    for copy in copies:
        copy.start()
    tail = pl.ds(pl.multiple_of((spans - 1) * SPAN, SPAN), SPAN)
    kf[tail, :] = jnp.zeros((SPAN, WIDTH), F32)
    vf[tail, :] = jnp.zeros((SPAN, WIDTH), F32)
    for copy in copies:
        copy.wait()

    @pl.loop(0, WINDOW)
    def _(j):
        w = sc[KEY_ORDER + j]
        rows = pl.ds(sc[KEY_OFFSET + w], SLOTS)
        kf[rows, :] = stage[w, 0].astype(F32)
        vf[rows, :] = stage[w, 1].astype(F32)

    def turn(n, longest):
        rows = pl.ds(pl.multiple_of(n * SPAN, SPAN), SPAN)
        keys = kf[rows, :].astype(BF16)
        vals = vf[rows, :].astype(BF16)
        kc[rows, :] = keys
        vc[rows, :] = vals
        keys = keys.T
        kt[n] = keys
        vt[n] = vals.T
        return jnp.maximum(longest, square(keys))

    long_ref[...] = lax.fori_loop(0, spans, turn, jnp.zeros((1, SPAN), F32))


def attend(sc, long_ref, rows_ref, *refs):
    keys_refs, (out_ref, near_ref, far_ref), scratch = refs[:4], refs[4:7], refs[7:]
    raw, kc, vc, kt, vt, qf, gf, of, dqf, thr, wb, wn, db, dk, dv, sems = scratch
    slot = slots()
    tiles = sc[TILE_COUNT]

    copies = [
        pltpu.make_async_copy(ref, place, sems.at[n])
        for n, (ref, place) in enumerate(zip((rows_ref, *keys_refs), (raw, kc, vc, kt, vt)))
    ]
    for copy in copies:
        copy.start()

    thr[tile_rows(tiles - 1), :] = jnp.full((SLOTS, WIDTH), -1, I32)

    @pl.loop(0, UNITS)
    def _(u):
        dk[unit_rows(u, UNIT), :] = jnp.zeros((UNIT, WIDTH), F32)
        dv[unit_rows(u, UNIT), :] = jnp.zeros((UNIT, WIDTH), F32)

    @pl.loop(0, SHARDS)
    def _(j):
        s = sc[QUERY_ORDER + j]
        thr[pl.ds(sc[QUERY_OFFSET + s], SLOTS), :] = jnp.where(
            slot < sc[QUERY_COUNT + s], slot + sc[QUERY_KEY + s], -1
        )

    longest = jnp.max(long_ref[...])
    copies[0].wait()
    pack_rows(sc, raw, 0, qf)
    pack_rows(sc, raw, 1, gf)
    for copy in copies[1:]:
        copy.wait()

    @pl.loop(0, tiles)
    def _(i):
        rows = tile_rows(i)
        count = up(sc[REACH + i], SPAN)
        limit = jnp.concatenate([thr[rows, :].T[0:1, :]] * HEADS, axis=1)
        q_tile = qf[:, rows, :].astype(BF16).reshape(LANES, WIDTH)
        q_turn = q_tile.T
        safe = jnp.max(square(q_turn)) * longest * BASE_TWO ** 2 <= SAFE ** 2

        def span_rows(n):
            return pl.ds(pl.multiple_of(n * SPAN, SPAN), SPAN)

        def scores(n):
            s = jnp.dot(kc[span_rows(n), :], q_turn, preferred_element_type=F32)
            return shown(s, n * SPAN, limit)

        top = lax.fori_loop(
            0,
            jnp.where(safe, 0, count),
            lambda n, top: jnp.maximum(top, fold(jnp.max, scores(n))),
            jnp.full((8, LANES), jnp.where(safe, 0.0, FLOOR), F32),
        )
        top = jnp.max(top, axis=0, keepdims=True) * BASE_TWO

        def weigh(n):
            w = jnp.exp2(scores(n) * BASE_TWO - top)
            low = w.astype(BF16)
            wb[span_rows(n), :] = low
            wn[...] = low
            return fold(jnp.sum, w)

        def mix(n):
            return jnp.dot(vt[n], wn[...], preferred_element_type=F32)

        def step(n, carry):
            total, acc = carry
            acc = acc + mix(n - 1)
            return total + weigh(n), acc

        total = weigh(0)
        total, acc = lax.fori_loop(1, count, step, (total, jnp.zeros((WIDTH, LANES), F32)))
        acc = acc + mix(count - 1)
        total = jnp.sum(total, axis=0, keepdims=True)
        inverse = 1.0 / jnp.where(total > 0.0, total, 1.0)
        out = (acc * inverse).astype(BF16)
        of[:, rows, :] = out.T.astype(F32).reshape(HEADS, SLOTS, WIDTH)

        g_turn = gf[:, rows, :].astype(BF16).reshape(LANES, WIDTH).T.astype(F32) * inverse
        g_turn = g_turn.astype(BF16)
        delta = jnp.sum(g_turn.astype(F32) * out.astype(F32), axis=0, keepdims=True)
        g_tile = g_turn.T

        def weigh_back(n):
            at = span_rows(n)
            dp = jnp.dot(vc[at, :], g_turn, preferred_element_type=F32)
            db[...] = (wb[at, :].astype(F32) * (dp - delta)).astype(BF16)

        def mix_back(n, acc):
            at = span_rows(n)
            dv[at, :] += jnp.dot(wb[at, :], g_tile, preferred_element_type=F32)
            dk[at, :] += jnp.dot(db[...], q_tile, preferred_element_type=F32)
            return acc + jnp.dot(kt[n], db[...], preferred_element_type=F32)

        def step_back(n, acc):
            acc = mix_back(n - 1, acc)
            weigh_back(n)
            return acc

        weigh_back(0)
        acc = lax.fori_loop(1, count, step_back, jnp.zeros((WIDTH, LANES), F32))
        acc = mix_back(count - 1, acc)
        dqf[:, rows, :] = (acc * SCALE).astype(BF16).T.astype(F32).reshape(HEADS, SLOTS, WIDTH)

    unpack_rows(sc, of, out_ref, 0)
    unpack_rows(sc, dqf, out_ref, 1)
    for g in range(2):
        for far in range(2):
            ref = far_ref if far else near_ref

            @pl.loop(0, 2 * N_X)
            def _(e, g=g, far=far, ref=ref):
                y, x = e // N_X, e % N_X
                w = g * 16 + far * 8 + e
                rows = pl.ds(sc[KEY_OFFSET + w], SLOTS)
                live = slot < sc[KEY_COUNT + w]
                ref[g, y, x, 0] = jnp.where(live, dk[rows, :] * SCALE, 0.0).astype(BF16)
                ref[g, y, x, 1] = jnp.where(live, dv[rows, :], 0.0).astype(BF16)


ROWS = (SHARDS, 2, HEADS, SLOTS, WIDTH)
KEYS = (KEY_ROWS, WIDTH)
TURNED_KEYS = (KEY_ROWS // SPAN, WIDTH, SPAN)
PACKING_KEYS = pltpu.VMEM((KEY_ROWS + SLOTS, WIDTH), F32)
PACKING_ROWS = pltpu.VMEM((HEADS, QUERY_ROWS + SLOTS, WIDTH), F32)


def call(kernel, operands, spaces, out_shape, scratch, flops, name):
    return pl.pallas_call(
        kernel,
        out_shape=out_shape,
        in_specs=[pl.BlockSpec(memory_space=space) for space in spaces],
        out_specs=(pl.BlockSpec(memory_space=pltpu.VMEM),) * len(out_shape),
        scratch_shapes=scratch,
        compiler_params=pltpu.CompilerParams(vmem_limit_bytes=56 * 1024 * 1024),
        cost_estimate=pl.CostEstimate(flops=flops, bytes_accessed=6 << 20, transcendentals=0),
        name=name,
    )(*operands)


def prepare_keys(scalars, pieces):
    shape = jax.ShapeDtypeStruct
    return call(
        prepare,
        (scalars, *pieces),
        (pltpu.SMEM,) + (pltpu.HBM,) * PIECES,
        (
            shape(KEYS, BF16),
            shape(KEYS, BF16),
            shape(TURNED_KEYS, BF16),
            shape(TURNED_KEYS, BF16),
            shape((1, SPAN), F32),
        ),
        [
            pltpu.VMEM((WINDOW, 2, SLOTS, WIDTH), BF16),
            PACKING_KEYS,
            PACKING_KEYS,
            pltpu.SemaphoreType.DMA((PIECES,)),
        ],
        1 << 20,
        "window_keys",
    )


def attention(scalars, rows, packed):
    *keys, longest = packed
    terms = jax.ShapeDtypeStruct((2, 2, N_X, 2, SLOTS, WIDTH), BF16)
    return call(
        attend,
        (scalars, longest, rows, *keys),
        (pltpu.SMEM, pltpu.VMEM) + (pltpu.HBM,) * 5,
        (jax.ShapeDtypeStruct(ROWS, BF16), terms, terms),
        [
            pltpu.VMEM(ROWS, BF16),
            *[pltpu.VMEM(KEYS, BF16)] * 2,
            *[pltpu.VMEM(TURNED_KEYS, BF16)] * 2,
            *[PACKING_ROWS] * 4,
            pltpu.VMEM((QUERY_ROWS + SLOTS, WIDTH), I32),
            pltpu.VMEM((KEY_ROWS, LANES), BF16),
            pltpu.VMEM((SPAN, LANES), BF16),
            pltpu.VMEM((SPAN, LANES), BF16),
            *[PACKING_KEYS] * 2,
            pltpu.SemaphoreType.DMA((5,)),
        ],
        20 << 30,
        "window_attention",
    )


def plan(kept_offset, region_pos):
    outer, y, x_, core = (lax.axis_index(a) for a in ("outer", "y", "x", "core"))
    shard = jnp.arange(N_OUTER * N_Y * N_X * N_CORE)
    counts = jnp.sum((kept_offset < REGION).astype(jnp.int32), axis=1)

    def pick(ids):
        hit = ids[:, None] == shard[None, :]
        of = lambda a: jnp.sum(jnp.where(hit, a[None, :], 0), axis=1)
        return of(counts), of(region_pos)

    w = jnp.arange(WINDOW)
    g, p, x = w // 16, w // 4 % 4, (x_ - w) % 4
    group = jnp.where(g == 0, outer, (outer - 1) % N_OUTER)
    count, place = pick(
        group * 16 + ((y ^ (p % 2)) * N_X + x) * N_CORE + (core ^ (p // 2))
    )
    before = place[None, :] < place[:, None]
    offset = jnp.sum(jnp.where(before, count[None, :], 0), axis=1)
    rank = jnp.sum(before.astype(jnp.int32), axis=1)
    order = jnp.sum(jnp.where(rank[None, :] == w[:, None], w[None, :], 0), axis=1)

    s = jnp.arange(SHARDS)
    q_count, q_place = pick(outer * 16 + (y * N_X + s // 2) * N_CORE + s % 2)
    q_before = q_place[None, :] < q_place[:, None]
    q_offset = jnp.sum(jnp.where(q_before, q_count[None, :], 0), axis=1)
    q_rank = jnp.sum(q_before.astype(jnp.int32), axis=1)
    q_order = jnp.sum(jnp.where(q_rank[None, :] == s[:, None], s[None, :], 0), axis=1)
    q_key = jnp.sum(jnp.where(place[None, :] < q_place[:, None], count[None, :], 0), axis=1)

    start = jnp.arange(TILES)[:, None] * SLOTS
    within = (q_offset[None, :] < start + SLOTS) & (q_offset[None, :] + q_count[None, :] > start)
    end = q_key[None, :] + jnp.minimum(q_count[None, :], start + SLOTS - q_offset[None, :])
    reach = jnp.max(jnp.where(within, end, 0), axis=1)
    tiles = (jnp.sum(q_count) + SLOTS - 1) // SLOTS

    pad = lambda a, n: jnp.pad(a, (0, n - a.shape[0]))
    return jnp.concatenate([
        order, offset, count,
        pad(q_order, 16), pad(q_offset, 16), pad(q_count, 16), pad(q_key, 16), pad(reach, 16),
        tiles[None],
    ]).astype(jnp.int32)


def total(*parts):
    return functools.reduce(jnp.add, [a.astype(F32) for a in parts]).astype(BF16)


def to_x(block, step):
    return lax.ppermute(block, "x", [(i, (i + step) % N_X) for i in range(N_X)])


def to_core(block):
    return lax.ppermute(block, "core", [(0, 1), (1, 0)])


def to_group(block, step, flip):
    route = [
        (i * 2 + y, (i + step) % N_OUTER * 2 + (y ^ flip))
        for i in range(N_OUTER)
        for y in range(N_Y)
    ]
    return lax.ppermute(block, ("outer", "y"), route)


def on_device(queries, keys, values, output_gradient, kept_offset, region_pos):
    x = lax.axis_index("x")
    exchange = functools.partial(lax.all_to_all, split_axis=0, concat_axis=0, tiled=True)
    kv = jnp.stack([keys, values]).transpose(2, 0, 1, 3)
    kv = [lax.dynamic_index_in_dim(kv, (x + k) % N_X, 0, keepdims=False) for k in range(N_X)]
    own = jnp.stack([to_x(kv[k], k) if k else kv[0] for k in range(N_X)])

    def by_head(a):
        return a.transpose(1, 0, 2).reshape(SHARDS, HEADS, SLOTS, WIDTH)

    rows = jnp.stack([by_head(queries), by_head(output_gradient)], axis=1)
    own, rows, kept_offset, region_pos = lax.optimization_barrier(
        (own, rows, kept_offset, region_pos)
    )
    scalars = plan(kept_offset, region_pos)
    own_pair = (own, to_group(own, 0, 1))
    prev_pair = (to_group(own, 1, 0), to_group(own, 1, 1))
    pieces = (
        *own_pair, *(to_core(a) for a in own_pair), *prev_pair, *(to_core(a) for a in prev_pair)
    )

    rows = exchange(rows, QUERY_AXES)
    rows, near, far = attention(scalars, rows, prepare_keys(scalars, pieces))
    far = to_core(far)
    term = lambda g, y: total(near[g, y], far[g, y])
    sums = total(
        term(0, 0),
        to_group(term(0, 1), 0, 1),
        to_group(term(1, 0), -1, 0),
        to_group(term(1, 1), -1, 1),
    )
    grads = [to_x(sums[k], -k) if k else sums[0] for k in range(N_X)]
    grads = jnp.stack([lax.select_n((h - x) % N_X, *grads) for h in range(N_X)])
    home = exchange(rows, QUERY_AXES)

    def by_slot(a):
        return a.reshape(HEADS_Q, SLOTS, WIDTH).transpose(1, 0, 2)

    return (
        by_slot(home[:, 0]),
        by_slot(home[:, 1]),
        grads[:, 0].transpose(1, 0, 2),
        grads[:, 1].transpose(1, 0, 2),
    )


def solution(mesh):
    devices = mesh.devices.reshape(N_OUTER, N_Y, N_X, N_CORE)
    split = Mesh(devices, ("outer", "y", "x", "core"))
    rows = P(("outer", "y", "x", "core"), None, None)
    return jax.shard_map(
        on_device,
        mesh=split,
        in_specs=(rows, rows, rows, rows, P(), P()),
        out_specs=(rows, rows, rows, rows),
        check_vma=False,
    )
```

```python
import functools
import math

import jax
import jax.numpy as jnp
from jax import lax
from jax.experimental import pallas as pl
from jax.experimental.pallas import tpu as pltpu
from jax.sharding import Mesh
from jax.sharding import PartitionSpec as P

REGION = 1024
SLOTS = 128
WIDTH = 128
HEADS_Q = 32
HEADS_KV = 4
N_OUTER = 16
N_Y = 2
N_X = 4
N_CORE = 2
WINDOW = 32
KEY_ROWS = WINDOW * SLOTS
PIECES = 8

QUERY_AXES = ("x", "core")
SHARDS = N_X * N_CORE
HEADS = HEADS_Q // SHARDS
QUERY_ROWS = SHARDS * SLOTS
TILES = SHARDS
LANES = HEADS * SLOTS
UNIT = 256
SPAN = 512
UNITS = KEY_ROWS // UNIT
SAFE = 60.0

FILL = -1e30
FLOOR = -1e29
SCALE = WIDTH ** (-0.5)
BASE_TWO = SCALE * math.log2(math.e)
BF16, F32, I32 = jnp.bfloat16, jnp.float32, jnp.int32

KEY_ORDER = 0
KEY_OFFSET = 32
KEY_COUNT = 64
QUERY_ORDER = 96
QUERY_OFFSET = 112
QUERY_COUNT = 128
QUERY_KEY = 144
REACH = 160
TILE_COUNT = 176


def slots():
    return lax.broadcasted_iota(I32, (SLOTS, WIDTH), 0)


def up(n, unit):
    return (n + unit - 1) // unit


def tile_rows(i):
    return pl.ds(pl.multiple_of(i * SLOTS, SLOTS), SLOTS)


def unit_rows(u, rows):
    return pl.ds(pl.multiple_of(u * UNIT, UNIT), rows)


def pack_rows(sc, array, part, packed):
    slot = slots()
    packed[:, tile_rows(sc[TILE_COUNT] - 1), :] = jnp.zeros((HEADS, SLOTS, WIDTH), F32)

    @pl.loop(0, SHARDS)
    def _(j):
        s = sc[QUERY_ORDER + j]
        live = (slot < sc[QUERY_COUNT + s])[None]
        packed[:, pl.ds(sc[QUERY_OFFSET + s], SLOTS), :] = jnp.where(
            live, array[s, part].astype(F32), 0.0
        )


def unpack_rows(sc, packed, array, part):
    slot = slots()

    @pl.loop(0, SHARDS)
    def _(s):
        live = (slot < sc[QUERY_COUNT + s])[None]
        rows = packed[:, pl.ds(sc[QUERY_OFFSET + s], SLOTS), :]
        array[s, part] = jnp.where(live, rows, 0.0).astype(BF16)


def shown(s, first, limit):
    place = lax.broadcasted_iota(I32, s.shape, 0)
    return jnp.where(place <= limit - first, s, FILL)


def fold(op, s):
    return op(s.reshape(-1, 8, s.shape[1]), axis=0)


def square(a):
    a = a.astype(F32)
    return jnp.sum(a * a, axis=0, keepdims=True)


def prepare(sc, *refs):
    pieces, (kc, vc, kt, vt, long_ref, stage, kf, vf, sems) = refs[:PIECES], refs[PIECES:]
    spans = up(sc[REACH + sc[TILE_COUNT] - 1], SPAN)
    copies = [
        pltpu.make_async_copy(ref, stage.at[pl.ds(p * N_X, N_X)], sems.at[p])
        for p, ref in enumerate(pieces)
    ]
    for copy in copies:
        copy.start()
    tail = pl.ds(pl.multiple_of((spans - 1) * SPAN, SPAN), SPAN)
    kf[tail, :] = jnp.zeros((SPAN, WIDTH), F32)
    vf[tail, :] = jnp.zeros((SPAN, WIDTH), F32)
    for copy in copies:
        copy.wait()

    @pl.loop(0, WINDOW)
    def _(j):
        w = sc[KEY_ORDER + j]
        rows = pl.ds(sc[KEY_OFFSET + w], SLOTS)
        kf[rows, :] = stage[w, 0].astype(F32)
        vf[rows, :] = stage[w, 1].astype(F32)

    def turn(n, longest):
        rows = pl.ds(pl.multiple_of(n * SPAN, SPAN), SPAN)
        keys = kf[rows, :].astype(BF16)
        vals = vf[rows, :].astype(BF16)
        kc[rows, :] = keys
        vc[rows, :] = vals
        keys = keys.T
        kt[n] = keys
        vt[n] = vals.T
        return jnp.maximum(longest, square(keys))

    long_ref[...] = lax.fori_loop(0, spans, turn, jnp.zeros((1, SPAN), F32))


def attend(sc, long_ref, rows_ref, *refs):
    keys_refs, (out_ref, *term_refs), scratch = refs[:4], refs[4:7], refs[7:]
    raw, kc, vc, kt, vt, qf, gf, thr, limits, qt, gt, ot, dqt = scratch[:13]
    wb, wn, db, dk, dv, terms, sems, out_sems = scratch[13:]
    slot = slots()
    tiles = sc[TILE_COUNT]

    copies = [
        pltpu.make_async_copy(ref, place, sems.at[n])
        for n, (ref, place) in enumerate(zip((rows_ref, *keys_refs), (raw, kc, vc, kt, vt)))
    ]
    for copy in copies:
        copy.start()

    thr[tile_rows(tiles - 1), :] = jnp.full((SLOTS, WIDTH), -1, I32)

    @pl.loop(0, UNITS)
    def _(u):
        dk[unit_rows(u, UNIT), :] = jnp.zeros((UNIT, WIDTH), F32)
        dv[unit_rows(u, UNIT), :] = jnp.zeros((UNIT, WIDTH), F32)

    @pl.loop(0, SHARDS)
    def _(j):
        s = sc[QUERY_ORDER + j]
        thr[pl.ds(sc[QUERY_OFFSET + s], SLOTS), :] = jnp.where(
            slot < sc[QUERY_COUNT + s], slot + sc[QUERY_KEY + s], -1
        )

    longest = jnp.max(long_ref[...])
    copies[0].wait()
    pack_rows(sc, raw, 0, qf)
    pack_rows(sc, raw, 1, gf)
    for copy in copies[1:]:
        copy.wait()

    def turn(i, longest_row):
        rows = tile_rows(i)
        limits[i] = jnp.concatenate([thr[rows, :].T[0:1, :]] * HEADS, axis=1)
        q_turn = qf[:, rows, :].astype(BF16).reshape(LANES, WIDTH).T
        qt[i] = q_turn
        gt[i] = gf[:, rows, :].astype(BF16).reshape(LANES, WIDTH).T
        return jnp.maximum(longest_row, square(q_turn))

    longest_row = jnp.max(lax.fori_loop(0, tiles, turn, jnp.zeros((1, LANES), F32)))
    safe = longest_row * longest * BASE_TWO ** 2 <= SAFE ** 2

    @pl.loop(0, tiles)
    def _(i):
        rows = tile_rows(i)
        count = up(sc[REACH + i], SPAN)
        limit = limits[i]
        q_turn = qt[i]

        def span_rows(n):
            return pl.ds(pl.multiple_of(n * SPAN, SPAN), SPAN)

        def scores(n):
            s = jnp.dot(kc[span_rows(n), :], q_turn, preferred_element_type=F32)
            return shown(s, n * SPAN, limit)

        top = lax.fori_loop(
            0,
            jnp.where(safe, 0, count),
            lambda n, top: jnp.maximum(top, fold(jnp.max, scores(n))),
            jnp.full((8, LANES), jnp.where(safe, 0.0, FLOOR), F32),
        )
        top = jnp.max(top, axis=0, keepdims=True) * BASE_TWO

        def weigh(n):
            w = jnp.exp2(scores(n) * BASE_TWO - top)
            low = w.astype(BF16)
            wb[span_rows(n), :] = low
            wn[...] = low
            return fold(jnp.sum, w)

        def mix(n):
            return jnp.dot(vt[n], wn[...], preferred_element_type=F32)

        def step(n, carry):
            total, acc = carry
            acc = acc + mix(n - 1)
            return total + weigh(n), acc

        total = weigh(0)
        total, acc = lax.fori_loop(1, count, step, (total, jnp.zeros((WIDTH, LANES), F32)))
        acc = acc + mix(count - 1)
        total = jnp.sum(total, axis=0, keepdims=True)
        inverse = 1.0 / jnp.where(total > 0.0, total, 1.0)
        out = (acc * inverse).astype(BF16)
        ot[i] = out

        g_turn = gt[i]
        delta = jnp.sum(g_turn.astype(F32) * out.astype(F32), axis=0, keepdims=True)
        by_row = jnp.stack([
            jnp.broadcast_to(inverse[:, h * SLOTS : (h + 1) * SLOTS], (SLOTS, SLOTS)).T
            for h in range(HEADS)
        ])
        q_tile = (qf[:, rows, :] * by_row).astype(BF16).reshape(LANES, WIDTH)
        g_tile = (gf[:, rows, :] * by_row).astype(BF16).reshape(LANES, WIDTH)

        def weigh_back(n):
            at = span_rows(n)
            dp = jnp.dot(vc[at, :], g_turn, preferred_element_type=F32)
            db[...] = (wb[at, :].astype(F32) * (dp - delta)).astype(BF16)

        def mix_back(n, acc):
            at = span_rows(n)
            dv[at, :] += jnp.dot(wb[at, :], g_tile, preferred_element_type=F32)
            dk[at, :] += jnp.dot(db[...], q_tile, preferred_element_type=F32)
            return acc + jnp.dot(kt[n], db[...], preferred_element_type=F32)

        def step_back(n, acc):
            acc = mix_back(n - 1, acc)
            weigh_back(n)
            return acc

        weigh_back(0)
        acc = lax.fori_loop(1, count, step_back, jnp.zeros((WIDTH, LANES), F32))
        acc = mix_back(count - 1, acc)
        dqt[i] = (acc * (inverse * SCALE)).astype(BF16)

    out_copies = [
        pltpu.make_async_copy(terms.at[far], term_refs[far], out_sems.at[far]) for far in range(2)
    ]
    out_copies += [
        pltpu.make_async_copy(raw.at[:, part], out_ref.at[:, part], out_sems.at[2 + part])
        for part in range(2)
    ]
    for far in range(2):
        for g in range(2):

            @pl.loop(0, 2 * N_X)
            def _(e, g=g, far=far):
                y, x = e // N_X, e % N_X
                w = g * 16 + far * 8 + e
                rows = pl.ds(sc[KEY_OFFSET + w], SLOTS)
                live = slot < sc[KEY_COUNT + w]
                terms[far, g, y, x, 0] = jnp.where(live, dk[rows, :] * SCALE, 0.0).astype(BF16)
                terms[far, g, y, x, 1] = jnp.where(live, dv[rows, :], 0.0).astype(BF16)

        out_copies[far].start()

    for part, (turned, packed) in enumerate(((ot, qf), (dqt, gf))):

        @pl.loop(0, tiles)
        def _(i, turned=turned, packed=packed):
            rows = turned[i].T.astype(F32).reshape(HEADS, SLOTS, WIDTH)
            packed[:, tile_rows(i), :] = rows

        unpack_rows(sc, packed, raw, part)
        out_copies[2 + part].start()

    for copy in out_copies:
        copy.wait()


ROWS = (SHARDS, 2, HEADS, SLOTS, WIDTH)
KEYS = (KEY_ROWS, WIDTH)
TURNED_KEYS = (KEY_ROWS // SPAN, WIDTH, SPAN)
PACKING_KEYS = pltpu.VMEM((KEY_ROWS + SLOTS, WIDTH), F32)
PACKING_ROWS = pltpu.VMEM((HEADS, QUERY_ROWS + SLOTS, WIDTH), F32)


def call(kernel, operands, spaces, out_shape, out_space, scratch, flops, limit, name):
    return pl.pallas_call(
        kernel,
        out_shape=out_shape,
        in_specs=[pl.BlockSpec(memory_space=space) for space in spaces],
        out_specs=(pl.BlockSpec(memory_space=out_space),) * len(out_shape),
        scratch_shapes=scratch,
        compiler_params=pltpu.CompilerParams(vmem_limit_bytes=limit << 20),
        cost_estimate=pl.CostEstimate(flops=flops, bytes_accessed=6 << 20, transcendentals=0),
        name=name,
    )(*operands)


def prepare_keys(scalars, pieces):
    shape = jax.ShapeDtypeStruct
    return call(
        prepare,
        (scalars, *pieces),
        (pltpu.SMEM,) + (pltpu.HBM,) * PIECES,
        (
            shape(KEYS, BF16),
            shape(KEYS, BF16),
            shape(TURNED_KEYS, BF16),
            shape(TURNED_KEYS, BF16),
            shape((1, SPAN), F32),
        ),
        pltpu.VMEM,
        [
            pltpu.VMEM((WINDOW, 2, SLOTS, WIDTH), BF16),
            PACKING_KEYS,
            PACKING_KEYS,
            pltpu.SemaphoreType.DMA((PIECES,)),
        ],
        1 << 20,
        56,
        "window_keys",
    )


def attention(scalars, rows, packed):
    *keys, longest = packed
    terms = jax.ShapeDtypeStruct((2, 2, N_X, 2, SLOTS, WIDTH), BF16)
    return call(
        attend,
        (scalars, longest, rows, *keys),
        (pltpu.SMEM, pltpu.VMEM, pl.ANY) + (pltpu.HBM,) * 4,
        (jax.ShapeDtypeStruct(ROWS, BF16), terms, terms),
        pltpu.HBM,
        [
            pltpu.VMEM(ROWS, BF16),
            *[pltpu.VMEM(KEYS, BF16)] * 2,
            *[pltpu.VMEM(TURNED_KEYS, BF16)] * 2,
            *[PACKING_ROWS] * 2,
            pltpu.VMEM((QUERY_ROWS + SLOTS, WIDTH), I32),
            pltpu.VMEM((TILES, 1, LANES), I32),
            *[pltpu.VMEM((TILES, WIDTH, LANES), BF16)] * 4,
            pltpu.VMEM((KEY_ROWS, LANES), BF16),
            pltpu.VMEM((SPAN, LANES), BF16),
            pltpu.VMEM((SPAN, LANES), BF16),
            *[PACKING_KEYS] * 2,
            pltpu.VMEM((2, *terms.shape), BF16),
            pltpu.SemaphoreType.DMA((5,)),
            pltpu.SemaphoreType.DMA((4,)),
        ],
        20 << 30,
        42,
        "window_attention",
    )


def plan(kept_offset, region_pos):
    outer, y, x_, core = (lax.axis_index(a) for a in ("outer", "y", "x", "core"))
    shard = jnp.arange(N_OUTER * N_Y * N_X * N_CORE)
    counts = jnp.sum((kept_offset < REGION).astype(jnp.int32), axis=1)

    def pick(ids):
        hit = ids[:, None] == shard[None, :]
        of = lambda a: jnp.sum(jnp.where(hit, a[None, :], 0), axis=1)
        return of(counts), of(region_pos)

    w = jnp.arange(WINDOW)
    g, p, x = w // 16, w // 4 % 4, (x_ - w) % 4
    group = jnp.where(g == 0, outer, (outer - 1) % N_OUTER)
    count, place = pick(
        group * 16 + ((y ^ (p % 2)) * N_X + x) * N_CORE + (core ^ (p // 2))
    )
    before = place[None, :] < place[:, None]
    offset = jnp.sum(jnp.where(before, count[None, :], 0), axis=1)
    rank = jnp.sum(before.astype(jnp.int32), axis=1)
    order = jnp.sum(jnp.where(rank[None, :] == w[:, None], w[None, :], 0), axis=1)

    s = jnp.arange(SHARDS)
    q_count, q_place = pick(outer * 16 + (y * N_X + s // 2) * N_CORE + s % 2)
    q_before = q_place[None, :] < q_place[:, None]
    q_offset = jnp.sum(jnp.where(q_before, q_count[None, :], 0), axis=1)
    q_rank = jnp.sum(q_before.astype(jnp.int32), axis=1)
    q_order = jnp.sum(jnp.where(q_rank[None, :] == s[:, None], s[None, :], 0), axis=1)
    q_key = jnp.sum(jnp.where(place[None, :] < q_place[:, None], count[None, :], 0), axis=1)

    start = jnp.arange(TILES)[:, None] * SLOTS
    within = (q_offset[None, :] < start + SLOTS) & (q_offset[None, :] + q_count[None, :] > start)
    end = q_key[None, :] + jnp.minimum(q_count[None, :], start + SLOTS - q_offset[None, :])
    reach = jnp.max(jnp.where(within, end, 0), axis=1)
    tiles = (jnp.sum(q_count) + SLOTS - 1) // SLOTS

    pad = lambda a, n: jnp.pad(a, (0, n - a.shape[0]))
    return jnp.concatenate([
        order, offset, count,
        pad(q_order, 16), pad(q_offset, 16), pad(q_count, 16), pad(q_key, 16), pad(reach, 16),
        tiles[None],
    ]).astype(jnp.int32)


def total(*parts):
    return functools.reduce(jnp.add, [a.astype(F32) for a in parts]).astype(BF16)


def to_x(block, step):
    return lax.ppermute(block, "x", [(i, (i + step) % N_X) for i in range(N_X)])


def to_core(block):
    return lax.ppermute(block, "core", [(0, 1), (1, 0)])


def to_group(block, step, flip):
    route = [
        (i * 2 + y, (i + step) % N_OUTER * 2 + (y ^ flip))
        for i in range(N_OUTER)
        for y in range(N_Y)
    ]
    return lax.ppermute(block, ("outer", "y"), route)


def on_device(queries, keys, values, output_gradient, kept_offset, region_pos):
    x = lax.axis_index("x")
    exchange = functools.partial(lax.all_to_all, split_axis=0, concat_axis=0, tiled=True)
    kv = jnp.stack([keys, values]).transpose(2, 0, 1, 3)
    kv = [lax.dynamic_index_in_dim(kv, (x + k) % N_X, 0, keepdims=False) for k in range(N_X)]
    own = jnp.stack([to_x(kv[k], k) if k else kv[0] for k in range(N_X)])

    def by_head(a):
        return a.transpose(1, 0, 2).reshape(SHARDS, HEADS, SLOTS, WIDTH)

    rows = jnp.stack([by_head(queries), by_head(output_gradient)], axis=1)
    own, rows, kept_offset, region_pos = lax.optimization_barrier(
        (own, rows, kept_offset, region_pos)
    )
    scalars = plan(kept_offset, region_pos)
    own_pair = (own, to_group(own, 0, 1))
    prev_pair = (to_group(own, 1, 0), to_group(own, 1, 1))
    pieces = (
        *own_pair, *(to_core(a) for a in own_pair), *prev_pair, *(to_core(a) for a in prev_pair)
    )

    rows = exchange(rows, QUERY_AXES)
    rows, near, far = attention(scalars, rows, prepare_keys(scalars, pieces))
    far = to_core(far)
    term = lambda g, y: total(near[g, y], far[g, y])
    sums = total(
        term(0, 0),
        to_group(term(0, 1), 0, 1),
        to_group(term(1, 0), -1, 0),
        to_group(term(1, 1), -1, 1),
    )
    grads = [to_x(sums[k], -k) if k else sums[0] for k in range(N_X)]
    grads = jnp.stack([lax.select_n((h - x) % N_X, *grads) for h in range(N_X)])
    home = exchange(rows, QUERY_AXES)

    def by_slot(a):
        return a.reshape(HEADS_Q, SLOTS, WIDTH).transpose(1, 0, 2)

    return (
        by_slot(home[:, 0]),
        by_slot(home[:, 1]),
        grads[:, 0].transpose(1, 0, 2),
        grads[:, 1].transpose(1, 0, 2),
    )


def solution(mesh):
    devices = mesh.devices.reshape(N_OUTER, N_Y, N_X, N_CORE)
    split = Mesh(devices, ("outer", "y", "x", "core"))
    rows = P(("outer", "y", "x", "core"), None, None)
    return jax.shard_map(
        on_device,
        mesh=split,
        in_specs=(rows, rows, rows, rows, P(), P()),
        out_specs=(rows, rows, rows, rows),
        check_vma=False,
    )
```

```python
import functools
import math

import jax
import jax.numpy as jnp
from jax import lax
from jax.experimental import pallas as pl
from jax.experimental.pallas import tpu as pltpu
from jax.sharding import Mesh
from jax.sharding import PartitionSpec as P

REGION = 1024
SLOTS = 128
WIDTH = 128
HEADS_Q = 32
HEADS_KV = 4
N_OUTER = 16
N_Y = 2
N_X = 4
N_CORE = 2
WINDOW = 32
KEY_ROWS = WINDOW * SLOTS
PIECES = 8

QUERY_AXES = ("x", "core")
SHARDS = N_X * N_CORE
HEADS = HEADS_Q // SHARDS
QUERY_ROWS = SHARDS * SLOTS
TILES = SHARDS
LANES = HEADS * SLOTS
UNIT = 256
SPAN = 512
UNITS = KEY_ROWS // UNIT
SAFE = 60.0

FILL = -1e30
FLOOR = -1e29
SCALE = WIDTH ** (-0.5)
BASE_TWO = SCALE * math.log2(math.e)
BF16, F32, I32 = jnp.bfloat16, jnp.float32, jnp.int32

KEY_ORDER = 0
KEY_OFFSET = 32
KEY_COUNT = 64
QUERY_ORDER = 96
QUERY_OFFSET = 112
QUERY_COUNT = 128
QUERY_KEY = 144
REACH = 160
TILE_COUNT = 176


def slots():
    return lax.broadcasted_iota(I32, (SLOTS, WIDTH), 0)


def up(n, unit):
    return (n + unit - 1) // unit


def tile_rows(i):
    return pl.ds(pl.multiple_of(i * SLOTS, SLOTS), SLOTS)


def unit_rows(u, rows):
    return pl.ds(pl.multiple_of(u * UNIT, UNIT), rows)


def pack_rows(sc, array, part, packed):
    slot = slots()
    packed[:, tile_rows(sc[TILE_COUNT] - 1), :] = jnp.zeros((HEADS, SLOTS, WIDTH), F32)

    @pl.loop(0, SHARDS)
    def _(j):
        s = sc[QUERY_ORDER + j]
        live = (slot < sc[QUERY_COUNT + s])[None]
        packed[:, pl.ds(sc[QUERY_OFFSET + s], SLOTS), :] = jnp.where(
            live, array[s, part].astype(F32), 0.0
        )


def unpack_rows(sc, packed, array, part):
    slot = slots()

    @pl.loop(0, SHARDS)
    def _(s):
        live = (slot < sc[QUERY_COUNT + s])[None]
        rows = packed[:, pl.ds(sc[QUERY_OFFSET + s], SLOTS), :]
        array[s, part] = jnp.where(live, rows, 0.0).astype(BF16)


def shown(s, first, limit):
    place = lax.broadcasted_iota(I32, s.shape, 0)
    return jnp.where(place <= limit - first, s, FILL)


def fold(op, s):
    return op(s.reshape(-1, 8, s.shape[1]), axis=0)


def square(a):
    a = a.astype(F32)
    return jnp.sum(a * a, axis=0, keepdims=True)


def prepare(sc, *refs):
    pieces, out_refs, long_ref = refs[:PIECES], refs[PIECES : PIECES + 4], refs[PIECES + 4]
    kc, vc, kt, vt, longs, stage, kf, vf, sems, out_sems = refs[PIECES + 5 :]
    spans = up(sc[REACH + sc[TILE_COUNT] - 1], SPAN)
    copies = [
        pltpu.make_async_copy(ref, stage.at[pl.ds(p * N_X, N_X)], sems.at[p])
        for p, ref in enumerate(pieces)
    ]
    for copy in copies:
        copy.start()
    tail = pl.ds(pl.multiple_of((spans - 1) * SPAN, SPAN), SPAN)
    kf[tail, :] = jnp.zeros((SPAN, WIDTH), F32)
    vf[tail, :] = jnp.zeros((SPAN, WIDTH), F32)
    for copy in copies:
        copy.wait()

    @pl.loop(0, WINDOW)
    def _(j):
        w = sc[KEY_ORDER + j]
        rows = pl.ds(sc[KEY_OFFSET + w], SLOTS)
        kf[rows, :] = stage[w, 0].astype(F32)
        vf[rows, :] = stage[w, 1].astype(F32)

    def turn(n, longest):
        rows = pl.ds(pl.multiple_of(n * SPAN, SPAN), SPAN)
        keys = kf[rows, :].astype(BF16)
        vals = vf[rows, :].astype(BF16)
        kc[rows, :] = keys
        vc[rows, :] = vals
        keys = keys.T
        kt[n] = keys
        vt[n] = vals.T
        return jnp.maximum(longest, square(keys))

    longs[...] = lax.fori_loop(0, spans, turn, jnp.zeros((1, SPAN), F32))
    out_copies = [
        pltpu.make_async_copy(held, ref, out_sems.at[n])
        for n, (held, ref) in enumerate(zip((kc, vc, kt, vt, longs), (*out_refs, long_ref)))
    ]
    for copy in out_copies:
        copy.start()
    for copy in out_copies:
        copy.wait()


def attend(sc, long_ref, rows_ref, *refs):
    keys_refs, (out_ref, *term_refs), scratch = refs[:4], refs[4:7], refs[7:]
    raw, kc, vc, kt, vt, qf, gf, thr, limits, qt, gt, ot, dqt = scratch[:13]
    wb, wn, db, dk, dv, tops, terms, sems, out_sems = scratch[13:]
    slot = slots()
    tiles = sc[TILE_COUNT]

    copies = [
        pltpu.make_async_copy(ref, place, sems.at[n])
        for n, (ref, place) in enumerate(zip((rows_ref, *keys_refs), (raw, kc, vc, kt, vt)))
    ]
    for copy in copies:
        copy.start()

    thr[tile_rows(tiles - 1), :] = jnp.full((SLOTS, WIDTH), -1, I32)

    @pl.loop(0, UNITS)
    def _(u):
        dk[unit_rows(u, UNIT), :] = jnp.zeros((UNIT, WIDTH), F32)
        dv[unit_rows(u, UNIT), :] = jnp.zeros((UNIT, WIDTH), F32)

    @pl.loop(0, SHARDS)
    def _(j):
        s = sc[QUERY_ORDER + j]
        thr[pl.ds(sc[QUERY_OFFSET + s], SLOTS), :] = jnp.where(
            slot < sc[QUERY_COUNT + s], slot + sc[QUERY_KEY + s], -1
        )

    longest = jnp.max(long_ref[...])
    copies[0].wait()
    pack_rows(sc, raw, 0, qf)
    pack_rows(sc, raw, 1, gf)
    for copy in copies[1:]:
        copy.wait()

    def turn(i, longest_row):
        rows = tile_rows(i)
        limits[i] = jnp.concatenate([thr[rows, :].T[0:1, :]] * HEADS, axis=1)
        q_turn = qf[:, rows, :].astype(BF16).reshape(LANES, WIDTH).T
        qt[i] = q_turn
        gt[i] = gf[:, rows, :].astype(BF16).reshape(LANES, WIDTH).T
        return jnp.maximum(longest_row, square(q_turn))

    longest_row = jnp.max(lax.fori_loop(0, tiles, turn, jnp.zeros((1, LANES), F32)))
    safe = longest_row * longest * BASE_TWO ** 2 <= SAFE ** 2

    def span_rows(n):
        return pl.ds(pl.multiple_of(n * SPAN, SPAN), SPAN)

    def scores(i, n):
        s = jnp.dot(kc[span_rows(n), :], qt[i], preferred_element_type=F32)
        return shown(s, n * SPAN, limits[i])

    def weigh(i, n):
        w = jnp.exp2(scores(i, n) * BASE_TWO - tops[i])
        low = w.astype(BF16)
        wb[span_rows(n), :] = low
        wn[...] = low
        return fold(jnp.sum, w)

    @pl.loop(0, tiles)
    def _(i):
        top = lax.fori_loop(
            0,
            jnp.where(safe, 0, up(sc[REACH + i], SPAN)),
            lambda n, top: jnp.maximum(top, fold(jnp.max, scores(i, n))),
            jnp.full((8, LANES), jnp.where(safe, 0.0, FLOOR), F32),
        )
        tops[i] = jnp.max(top, axis=0, keepdims=True) * BASE_TWO

    def attend_tile(i, total):
        rows = tile_rows(i)
        count = up(sc[REACH + i], SPAN)

        def mix(n):
            return jnp.dot(vt[n], wn[...], preferred_element_type=F32)

        def step(n, carry):
            total, acc = carry
            acc = acc + mix(n - 1)
            return total + weigh(i, n), acc

        total, acc = lax.fori_loop(1, count, step, (total, jnp.zeros((WIDTH, LANES), F32)))
        acc = acc + mix(count - 1)
        total = jnp.sum(total, axis=0, keepdims=True)
        inverse = 1.0 / jnp.where(total > 0.0, total, 1.0)
        out = (acc * inverse).astype(BF16)
        ot[i] = out

        g_turn = gt[i]
        delta = jnp.sum(g_turn.astype(F32) * out.astype(F32), axis=0, keepdims=True)
        by_row = jnp.stack([
            jnp.broadcast_to(inverse[:, h * SLOTS : (h + 1) * SLOTS], (SLOTS, SLOTS)).T
            for h in range(HEADS)
        ])
        q_tile = (qf[:, rows, :] * by_row).astype(BF16).reshape(LANES, WIDTH)
        g_tile = (gf[:, rows, :] * by_row).astype(BF16).reshape(LANES, WIDTH)

        def weigh_back(n):
            at = span_rows(n)
            dp = jnp.dot(vc[at, :], g_turn, preferred_element_type=F32)
            db[...] = (wb[at, :].astype(F32) * (dp - delta)).astype(BF16)

        def mix_back(n, acc):
            at = span_rows(n)
            dv[at, :] += jnp.dot(wb[at, :], g_tile, preferred_element_type=F32)
            dk[at, :] += jnp.dot(db[...], q_tile, preferred_element_type=F32)
            return acc + jnp.dot(kt[n], db[...], preferred_element_type=F32)

        def step_back(n, acc):
            acc = mix_back(n - 1, acc)
            weigh_back(n)
            return acc

        weigh_back(0)
        acc = lax.fori_loop(1, count, step_back, jnp.zeros((WIDTH, LANES), F32))
        acc = mix_back(count - 1, acc)
        dqt[i] = (acc * (inverse * SCALE)).astype(BF16)
        return weigh(jnp.minimum(i + 1, tiles - 1), 0)

    lax.fori_loop(0, tiles, attend_tile, weigh(0, 0))

    out_copies = [
        pltpu.make_async_copy(terms.at[far], term_refs[far], out_sems.at[far]) for far in range(2)
    ]
    out_copies += [
        pltpu.make_async_copy(raw.at[:, part], out_ref.at[:, part], out_sems.at[2 + part])
        for part in range(2)
    ]
    for far in range(2):
        for g in range(2):

            @pl.loop(0, 2 * N_X)
            def _(e, g=g, far=far):
                y, x = e // N_X, e % N_X
                w = g * 16 + far * 8 + e
                rows = pl.ds(sc[KEY_OFFSET + w], SLOTS)
                live = slot < sc[KEY_COUNT + w]
                terms[far, g, y, x, 0] = jnp.where(live, dk[rows, :] * SCALE, 0.0).astype(BF16)
                terms[far, g, y, x, 1] = jnp.where(live, dv[rows, :], 0.0).astype(BF16)

        out_copies[far].start()

    for part, (turned, packed) in enumerate(((ot, qf), (dqt, gf))):

        @pl.loop(0, tiles)
        def _(i, turned=turned, packed=packed):
            rows = turned[i].T.astype(F32).reshape(HEADS, SLOTS, WIDTH)
            packed[:, tile_rows(i), :] = rows

        unpack_rows(sc, packed, raw, part)
        out_copies[2 + part].start()

    for copy in out_copies:
        copy.wait()


ROWS = (SHARDS, 2, HEADS, SLOTS, WIDTH)
KEYS = (KEY_ROWS, WIDTH)
TURNED_KEYS = (KEY_ROWS // SPAN, WIDTH, SPAN)
PACKING_KEYS = pltpu.VMEM((KEY_ROWS + SLOTS, WIDTH), F32)
PACKING_ROWS = pltpu.VMEM((HEADS, QUERY_ROWS + SLOTS, WIDTH), F32)


def call(kernel, operands, spaces, out_shape, out_space, scratch, flops, limit, name):
    return pl.pallas_call(
        kernel,
        out_shape=out_shape,
        in_specs=[pl.BlockSpec(memory_space=space) for space in spaces],
        out_specs=(pl.BlockSpec(memory_space=out_space),) * len(out_shape),
        scratch_shapes=scratch,
        compiler_params=pltpu.CompilerParams(vmem_limit_bytes=limit << 20),
        cost_estimate=pl.CostEstimate(flops=flops, bytes_accessed=6 << 20, transcendentals=0),
        name=name,
    )(*operands)


def prepare_keys(scalars, pieces):
    shape = jax.ShapeDtypeStruct
    return call(
        prepare,
        (scalars, *pieces),
        (pltpu.SMEM,) + (pltpu.HBM,) * PIECES,
        (
            shape(KEYS, BF16),
            shape(KEYS, BF16),
            shape(TURNED_KEYS, BF16),
            shape(TURNED_KEYS, BF16),
            shape((1, SPAN), F32),
        ),
        pltpu.HBM,
        [
            *[pltpu.VMEM(KEYS, BF16)] * 2,
            *[pltpu.VMEM(TURNED_KEYS, BF16)] * 2,
            pltpu.VMEM((1, SPAN), F32),
            pltpu.VMEM((WINDOW, 2, SLOTS, WIDTH), BF16),
            PACKING_KEYS,
            PACKING_KEYS,
            pltpu.SemaphoreType.DMA((PIECES,)),
            pltpu.SemaphoreType.DMA((5,)),
        ],
        1 << 20,
        42,
        "window_keys",
    )


def attention(scalars, rows, packed):
    *keys, longest = packed
    terms = jax.ShapeDtypeStruct((2, 2, N_X, 2, SLOTS, WIDTH), BF16)
    return call(
        attend,
        (scalars, longest, rows, *keys),
        (pltpu.SMEM, pltpu.VMEM, pl.ANY) + (pltpu.HBM,) * 4,
        (jax.ShapeDtypeStruct(ROWS, BF16), terms, terms),
        pltpu.HBM,
        [
            pltpu.VMEM(ROWS, BF16),
            *[pltpu.VMEM(KEYS, BF16)] * 2,
            *[pltpu.VMEM(TURNED_KEYS, BF16)] * 2,
            *[PACKING_ROWS] * 2,
            pltpu.VMEM((QUERY_ROWS + SLOTS, WIDTH), I32),
            pltpu.VMEM((TILES, 1, LANES), I32),
            *[pltpu.VMEM((TILES, WIDTH, LANES), BF16)] * 4,
            pltpu.VMEM((KEY_ROWS, LANES), BF16),
            pltpu.VMEM((SPAN, LANES), BF16),
            pltpu.VMEM((SPAN, LANES), BF16),
            *[PACKING_KEYS] * 2,
            pltpu.VMEM((TILES, 1, LANES), F32),
            pltpu.VMEM((2, *terms.shape), BF16),
            pltpu.SemaphoreType.DMA((5,)),
            pltpu.SemaphoreType.DMA((4,)),
        ],
        20 << 30,
        42,
        "window_attention",
    )


def plan(kept_offset, region_pos):
    outer, y, x_, core = (lax.axis_index(a) for a in ("outer", "y", "x", "core"))
    shard = jnp.arange(N_OUTER * N_Y * N_X * N_CORE)
    counts = jnp.sum((kept_offset < REGION).astype(jnp.int32), axis=1)

    def pick(ids):
        hit = ids[:, None] == shard[None, :]
        of = lambda a: jnp.sum(jnp.where(hit, a[None, :], 0), axis=1)
        return of(counts), of(region_pos)

    w = jnp.arange(WINDOW)
    g, p, x = w // 16, w // 4 % 4, (x_ - w) % 4
    group = jnp.where(g == 0, outer, (outer - 1) % N_OUTER)
    count, place = pick(
        group * 16 + ((y ^ (p % 2)) * N_X + x) * N_CORE + (core ^ (p // 2))
    )
    before = place[None, :] < place[:, None]
    offset = jnp.sum(jnp.where(before, count[None, :], 0), axis=1)
    rank = jnp.sum(before.astype(jnp.int32), axis=1)
    order = jnp.sum(jnp.where(rank[None, :] == w[:, None], w[None, :], 0), axis=1)

    s = jnp.arange(SHARDS)
    q_count, q_place = pick(outer * 16 + (y * N_X + s // 2) * N_CORE + s % 2)
    q_before = q_place[None, :] < q_place[:, None]
    q_offset = jnp.sum(jnp.where(q_before, q_count[None, :], 0), axis=1)
    q_rank = jnp.sum(q_before.astype(jnp.int32), axis=1)
    q_order = jnp.sum(jnp.where(q_rank[None, :] == s[:, None], s[None, :], 0), axis=1)
    q_key = jnp.sum(jnp.where(place[None, :] < q_place[:, None], count[None, :], 0), axis=1)

    start = jnp.arange(TILES)[:, None] * SLOTS
    within = (q_offset[None, :] < start + SLOTS) & (q_offset[None, :] + q_count[None, :] > start)
    end = q_key[None, :] + jnp.minimum(q_count[None, :], start + SLOTS - q_offset[None, :])
    reach = jnp.max(jnp.where(within, end, 0), axis=1)
    tiles = (jnp.sum(q_count) + SLOTS - 1) // SLOTS

    pad = lambda a, n: jnp.pad(a, (0, n - a.shape[0]))
    return jnp.concatenate([
        order, offset, count,
        pad(q_order, 16), pad(q_offset, 16), pad(q_count, 16), pad(q_key, 16), pad(reach, 16),
        tiles[None],
    ]).astype(jnp.int32)


def total(*parts):
    return functools.reduce(jnp.add, [a.astype(F32) for a in parts]).astype(BF16)


def to_x(block, step):
    return lax.ppermute(block, "x", [(i, (i + step) % N_X) for i in range(N_X)])


def to_core(block):
    return lax.ppermute(block, "core", [(0, 1), (1, 0)])


def to_group(block, step, flip):
    route = [
        (i * 2 + y, (i + step) % N_OUTER * 2 + (y ^ flip))
        for i in range(N_OUTER)
        for y in range(N_Y)
    ]
    return lax.ppermute(block, ("outer", "y"), route)


def on_device(queries, keys, values, output_gradient, kept_offset, region_pos):
    x = lax.axis_index("x")
    exchange = functools.partial(lax.all_to_all, split_axis=0, concat_axis=0, tiled=True)
    kv = jnp.stack([keys, values]).transpose(2, 0, 1, 3)
    kv = [lax.dynamic_index_in_dim(kv, (x + k) % N_X, 0, keepdims=False) for k in range(N_X)]
    own = jnp.stack([to_x(kv[k], k) if k else kv[0] for k in range(N_X)])

    def by_head(a):
        return a.transpose(1, 0, 2).reshape(SHARDS, HEADS, SLOTS, WIDTH)

    rows = jnp.stack([by_head(queries), by_head(output_gradient)], axis=1)
    own, rows, kept_offset, region_pos = lax.optimization_barrier(
        (own, rows, kept_offset, region_pos)
    )
    scalars = plan(kept_offset, region_pos)
    own_pair = (own, to_group(own, 0, 1))
    prev_pair = (to_group(own, 1, 0), to_group(own, 1, 1))
    pieces = (
        *own_pair, *(to_core(a) for a in own_pair), *prev_pair, *(to_core(a) for a in prev_pair)
    )

    rows = exchange(rows, QUERY_AXES)
    rows, near, far = attention(scalars, rows, prepare_keys(scalars, pieces))
    far = to_core(far)
    term = lambda g, y: total(near[g, y], far[g, y])
    sums = total(
        term(0, 0),
        to_group(term(0, 1), 0, 1),
        to_group(term(1, 0), -1, 0),
        to_group(term(1, 1), -1, 1),
    )
    grads = [to_x(sums[k], -k) if k else sums[0] for k in range(N_X)]
    home = exchange(rows, QUERY_AXES)

    def by_slot(a):
        return a.reshape(HEADS_Q, SLOTS, WIDTH).transpose(1, 0, 2)

    output, query_gradient = by_slot(home[:, 0]), by_slot(home[:, 1])
    output, query_gradient, grads = lax.optimization_barrier((output, query_gradient, grads))
    grads = jnp.stack([lax.select_n((h - x) % N_X, *grads) for h in range(N_X)])
    return (
        output,
        query_gradient,
        grads[:, 0].transpose(1, 0, 2),
        grads[:, 1].transpose(1, 0, 2),
    )


def solution(mesh):
    devices = mesh.devices.reshape(N_OUTER, N_Y, N_X, N_CORE)
    split = Mesh(devices, ("outer", "y", "x", "core"))
    rows = P(("outer", "y", "x", "core"), None, None)
    return jax.shard_map(
        on_device,
        mesh=split,
        in_specs=(rows, rows, rows, rows, P(), P()),
        out_specs=(rows, rows, rows, rows),
        check_vma=False,
    )
```

```python
import functools
import math

import jax
import jax.numpy as jnp
from jax import lax
from jax.experimental import pallas as pl
from jax.experimental.pallas import tpu as pltpu
from jax.sharding import Mesh
from jax.sharding import PartitionSpec as P

REGION = 1024
SLOTS = 128
WIDTH = 128
HEADS_Q = 32
HEADS_KV = 4
N_OUTER = 16
N_Y = 2
N_X = 4
N_CORE = 2
WINDOW = 32
KEY_ROWS = WINDOW * SLOTS
PIECES = 8

QUERY_AXES = ("x", "core")
SHARDS = N_X * N_CORE
HEADS = HEADS_Q // SHARDS
QUERY_ROWS = SHARDS * SLOTS
TILES = SHARDS
LANES = HEADS * SLOTS
UNIT = 256
SPAN = 512
UNITS = KEY_ROWS // UNIT
SAFE = 60.0

FILL = -1e30
FLOOR = -1e29
SCALE = WIDTH ** (-0.5)
BASE_TWO = SCALE * math.log2(math.e)
BF16, F32, I32 = jnp.bfloat16, jnp.float32, jnp.int32

KEY_ORDER = 0
KEY_OFFSET = 32
KEY_COUNT = 64
QUERY_ORDER = 96
QUERY_OFFSET = 112
QUERY_COUNT = 128
QUERY_KEY = 144
REACH = 160
TILE_COUNT = 176


def slots():
    return lax.broadcasted_iota(I32, (SLOTS, WIDTH), 0)


def up(n, unit):
    return (n + unit - 1) // unit


def tile_rows(i):
    return pl.ds(pl.multiple_of(i * SLOTS, SLOTS), SLOTS)


def unit_rows(u, rows):
    return pl.ds(pl.multiple_of(u * UNIT, UNIT), rows)


def pack_rows(sc, array, part, packed):
    slot = slots()
    packed[:, tile_rows(sc[TILE_COUNT] - 1), :] = jnp.zeros((HEADS, SLOTS, WIDTH), F32)

    @pl.loop(0, SHARDS)
    def _(j):
        s = sc[QUERY_ORDER + j]
        live = (slot < sc[QUERY_COUNT + s])[None]
        packed[:, pl.ds(sc[QUERY_OFFSET + s], SLOTS), :] = jnp.where(
            live, array[s, part].astype(F32), 0.0
        )


def unpack_rows(sc, packed, array, part):
    slot = slots()

    @pl.loop(0, SHARDS)
    def _(s):
        live = (slot < sc[QUERY_COUNT + s])[None]
        rows = packed[:, pl.ds(sc[QUERY_OFFSET + s], SLOTS), :]
        array[s, part] = jnp.where(live, rows, 0.0).astype(BF16)


def shown(s, first, limit):
    place = lax.broadcasted_iota(I32, s.shape, 0)
    return jnp.where(place <= limit - first, s, FILL)


def fold(op, s):
    return op(s.reshape(-1, 8, s.shape[1]), axis=0)


def square(a):
    a = a.astype(F32)
    return jnp.sum(a * a, axis=0, keepdims=True)


def prepare(sc, *refs):
    pieces, out_refs, long_ref = refs[:PIECES], refs[PIECES : PIECES + 4], refs[PIECES + 4]
    kc, vc, kt, vt, longs, stage, kf, vf, sems, out_sems = refs[PIECES + 5 :]
    spans = up(sc[REACH + sc[TILE_COUNT] - 1], SPAN)
    copies = [
        pltpu.make_async_copy(ref, stage.at[pl.ds(p * N_X, N_X)], sems.at[p])
        for p, ref in enumerate(pieces)
    ]
    for copy in copies:
        copy.start()
    tail = pl.ds(pl.multiple_of((spans - 1) * SPAN, SPAN), SPAN)
    kf[tail, :] = jnp.zeros((SPAN, WIDTH), F32)
    vf[tail, :] = jnp.zeros((SPAN, WIDTH), F32)
    for copy in copies:
        copy.wait()

    @pl.loop(0, WINDOW)
    def _(j):
        w = sc[KEY_ORDER + j]
        rows = pl.ds(sc[KEY_OFFSET + w], SLOTS)
        kf[rows, :] = stage[w, 0].astype(F32)
        vf[rows, :] = stage[w, 1].astype(F32)

    def turn(n, longest):
        rows = pl.ds(pl.multiple_of(n * SPAN, SPAN), SPAN)
        keys = kf[rows, :].astype(BF16)
        vals = vf[rows, :].astype(BF16)
        kc[rows, :] = keys
        vc[rows, :] = vals
        keys = keys.T
        kt[n] = keys
        vt[n] = vals.T
        return jnp.maximum(longest, square(keys))

    longs[...] = lax.fori_loop(0, spans, turn, jnp.zeros((1, SPAN), F32))
    out_copies = [
        pltpu.make_async_copy(held, ref, out_sems.at[n])
        for n, (held, ref) in enumerate(zip((kc, vc, kt, vt, longs), (*out_refs, long_ref)))
    ]
    for copy in out_copies:
        copy.start()
    for copy in out_copies:
        copy.wait()


def attend(sc, long_ref, rows_ref, *refs):
    keys_refs, (out_ref, *term_refs), scratch = refs[:4], refs[4:7], refs[7:]
    raw, kc, vc, kt, vt, qf, gf, thr, limits, qt, gt, ot, dqt = scratch[:13]
    wb, wn, db, dk, dv, tops, terms, sems, out_sems = scratch[13:]
    slot = slots()
    tiles = sc[TILE_COUNT]

    copies = [
        pltpu.make_async_copy(ref, place, sems.at[n])
        for n, (ref, place) in enumerate(zip((rows_ref, *keys_refs), (raw, kc, vc, kt, vt)))
    ]
    for copy in copies:
        copy.start()

    thr[tile_rows(tiles - 1), :] = jnp.full((SLOTS, WIDTH), -1, I32)

    @pl.loop(0, UNITS)
    def _(u):
        dk[unit_rows(u, UNIT), :] = jnp.zeros((UNIT, WIDTH), F32)
        dv[unit_rows(u, UNIT), :] = jnp.zeros((UNIT, WIDTH), F32)

    @pl.loop(0, SHARDS)
    def _(j):
        s = sc[QUERY_ORDER + j]
        thr[pl.ds(sc[QUERY_OFFSET + s], SLOTS), :] = jnp.where(
            slot < sc[QUERY_COUNT + s], slot + sc[QUERY_KEY + s], -1
        )

    longest = jnp.max(long_ref[...])
    copies[0].wait()
    pack_rows(sc, raw, 0, qf)
    pack_rows(sc, raw, 1, gf)
    for copy in copies[1:]:
        copy.wait()

    def turn(i, longest_row):
        rows = tile_rows(i)
        limits[i] = jnp.concatenate([thr[rows, :].T[0:1, :]] * HEADS, axis=1)
        q_turn = qf[:, rows, :].astype(BF16).reshape(LANES, WIDTH).T
        qt[i] = q_turn
        gt[i] = gf[:, rows, :].astype(BF16).reshape(LANES, WIDTH).T
        return jnp.maximum(longest_row, square(q_turn))

    longest_row = jnp.max(lax.fori_loop(0, tiles, turn, jnp.zeros((1, LANES), F32)))
    safe = longest_row * longest * BASE_TWO ** 2 <= SAFE ** 2

    def span_rows(n):
        return pl.ds(pl.multiple_of(n * SPAN, SPAN), SPAN)

    def scores(i, n):
        s = jnp.dot(kc[span_rows(n), :], qt[i], preferred_element_type=F32)
        return shown(s, n * SPAN, limits[i])

    def weigh(i, n):
        w = jnp.exp2(scores(i, n) * BASE_TWO - tops[i])
        low = w.astype(BF16)
        wb[span_rows(n), :] = low
        wn[...] = low
        return fold(jnp.sum, w)

    @pl.loop(0, tiles)
    def _(i):
        top = lax.fori_loop(
            0,
            jnp.where(safe, 0, up(sc[REACH + i], SPAN)),
            lambda n, top: jnp.maximum(top, fold(jnp.max, scores(i, n))),
            jnp.full((8, LANES), jnp.where(safe, 0.0, FLOOR), F32),
        )
        tops[i] = jnp.max(top, axis=0, keepdims=True) * BASE_TWO

    def attend_tile(i, total):
        rows = tile_rows(i)
        count = up(sc[REACH + i], SPAN)

        def mix(n):
            return jnp.dot(vt[n], wn[...], preferred_element_type=F32)

        def step(n, carry):
            total, acc = carry
            acc = acc + mix(n - 1)
            return total + weigh(i, n), acc

        total, acc = lax.fori_loop(1, count, step, (total, jnp.zeros((WIDTH, LANES), F32)))
        acc = acc + mix(count - 1)
        total = jnp.sum(total, axis=0, keepdims=True)
        inverse = 1.0 / jnp.where(total > 0.0, total, 1.0)
        out = (acc * inverse).astype(BF16)
        ot[i] = out

        g_turn = gt[i]
        delta = jnp.sum(g_turn.astype(F32) * out.astype(F32), axis=0, keepdims=True)
        by_row = jnp.stack([
            jnp.broadcast_to(inverse[:, h * SLOTS : (h + 1) * SLOTS], (SLOTS, SLOTS)).T
            for h in range(HEADS)
        ])
        q_tile = (qf[:, rows, :] * by_row).astype(BF16).reshape(LANES, WIDTH)
        g_tile = (gf[:, rows, :] * by_row).astype(BF16).reshape(LANES, WIDTH)

        def weigh_back(n):
            at = span_rows(n)
            dp = jnp.dot(vc[at, :], g_turn, preferred_element_type=F32)
            db[...] = (wb[at, :].astype(F32) * (dp - delta)).astype(BF16)

        def mix_back(n, acc):
            at = span_rows(n)
            dv[at, :] += jnp.dot(wb[at, :], g_tile, preferred_element_type=F32)
            dk[at, :] += jnp.dot(db[...], q_tile, preferred_element_type=F32)
            return acc + jnp.dot(kt[n], db[...], preferred_element_type=F32)

        def step_back(n, acc):
            acc = mix_back(n - 1, acc)
            weigh_back(n)
            return acc

        weigh_back(0)
        acc = lax.fori_loop(1, count, step_back, jnp.zeros((WIDTH, LANES), F32))
        acc = mix_back(count - 1, acc)
        dqt[i] = (acc * (inverse * SCALE)).astype(BF16)
        return weigh(jnp.minimum(i + 1, tiles - 1), 0)

    lax.fori_loop(0, tiles, attend_tile, weigh(0, 0))

    out_copies = [
        pltpu.make_async_copy(terms.at[far], term_refs[far], out_sems.at[far]) for far in range(2)
    ]
    out_copies += [
        pltpu.make_async_copy(raw.at[:, part], out_ref.at[:, part], out_sems.at[2 + part])
        for part in range(2)
    ]
    for far in range(2):
        for g in range(2):

            @pl.loop(0, 2 * N_X)
            def _(e, g=g, far=far):
                y, x = e // N_X, e % N_X
                w = g * 16 + far * 8 + e
                rows = pl.ds(sc[KEY_OFFSET + w], SLOTS)
                live = slot < sc[KEY_COUNT + w]
                terms[far, g, y, x, 0] = jnp.where(live, dk[rows, :] * SCALE, 0.0).astype(BF16)
                terms[far, g, y, x, 1] = jnp.where(live, dv[rows, :], 0.0).astype(BF16)

        out_copies[far].start()

    for part, (turned, packed) in enumerate(((ot, qf), (dqt, gf))):

        @pl.loop(0, tiles)
        def _(i, turned=turned, packed=packed):
            rows = turned[i].T.astype(F32).reshape(HEADS, SLOTS, WIDTH)
            packed[:, tile_rows(i), :] = rows

        unpack_rows(sc, packed, raw, part)
        out_copies[2 + part].start()

    for copy in out_copies:
        copy.wait()


ROWS = (SHARDS, 2, HEADS, SLOTS, WIDTH)
KEYS = (KEY_ROWS, WIDTH)
TURNED_KEYS = (KEY_ROWS // SPAN, WIDTH, SPAN)
PACKING_KEYS = pltpu.VMEM((KEY_ROWS + SLOTS, WIDTH), F32)
PACKING_ROWS = pltpu.VMEM((HEADS, QUERY_ROWS + SLOTS, WIDTH), F32)


def call(kernel, operands, spaces, out_shape, out_space, scratch, flops, limit, name):
    return pl.pallas_call(
        kernel,
        out_shape=out_shape,
        in_specs=[pl.BlockSpec(memory_space=space) for space in spaces],
        out_specs=(pl.BlockSpec(memory_space=out_space),) * len(out_shape),
        scratch_shapes=scratch,
        compiler_params=pltpu.CompilerParams(vmem_limit_bytes=limit << 20),
        cost_estimate=pl.CostEstimate(flops=flops, bytes_accessed=6 << 20, transcendentals=0),
        name=name,
    )(*operands)


def prepare_keys(scalars, pieces):
    shape = jax.ShapeDtypeStruct
    return call(
        prepare,
        (scalars, *pieces),
        (pltpu.SMEM,) + (pltpu.HBM,) * PIECES,
        (
            shape(KEYS, BF16),
            shape(KEYS, BF16),
            shape(TURNED_KEYS, BF16),
            shape(TURNED_KEYS, BF16),
            shape((1, SPAN), F32),
        ),
        pltpu.HBM,
        [
            *[pltpu.VMEM(KEYS, BF16)] * 2,
            *[pltpu.VMEM(TURNED_KEYS, BF16)] * 2,
            pltpu.VMEM((1, SPAN), F32),
            pltpu.VMEM((WINDOW, 2, SLOTS, WIDTH), BF16),
            PACKING_KEYS,
            PACKING_KEYS,
            pltpu.SemaphoreType.DMA((PIECES,)),
            pltpu.SemaphoreType.DMA((5,)),
        ],
        1 << 20,
        56,
        "window_keys",
    )


def attention(scalars, rows, packed):
    *keys, longest = packed
    terms = jax.ShapeDtypeStruct((2, 2, N_X, 2, SLOTS, WIDTH), BF16)
    return call(
        attend,
        (scalars, longest, rows, *keys),
        (pltpu.SMEM, pltpu.VMEM, pl.ANY) + (pltpu.HBM,) * 4,
        (jax.ShapeDtypeStruct(ROWS, BF16), terms, terms),
        pltpu.HBM,
        [
            pltpu.VMEM(ROWS, BF16),
            *[pltpu.VMEM(KEYS, BF16)] * 2,
            *[pltpu.VMEM(TURNED_KEYS, BF16)] * 2,
            *[PACKING_ROWS] * 2,
            pltpu.VMEM((QUERY_ROWS + SLOTS, WIDTH), I32),
            pltpu.VMEM((TILES, 1, LANES), I32),
            *[pltpu.VMEM((TILES, WIDTH, LANES), BF16)] * 4,
            pltpu.VMEM((KEY_ROWS, LANES), BF16),
            pltpu.VMEM((SPAN, LANES), BF16),
            pltpu.VMEM((SPAN, LANES), BF16),
            *[PACKING_KEYS] * 2,
            pltpu.VMEM((TILES, 1, LANES), F32),
            pltpu.VMEM((2, *terms.shape), BF16),
            pltpu.SemaphoreType.DMA((5,)),
            pltpu.SemaphoreType.DMA((4,)),
        ],
        20 << 30,
        56,
        "window_attention",
    )


def plan(kept_offset, region_pos):
    outer, y, x_, core = (lax.axis_index(a) for a in ("outer", "y", "x", "core"))
    shard = jnp.arange(N_OUTER * N_Y * N_X * N_CORE)
    counts = jnp.sum((kept_offset < REGION).astype(jnp.int32), axis=1)

    def pick(ids):
        hit = ids[:, None] == shard[None, :]
        of = lambda a: jnp.sum(jnp.where(hit, a[None, :], 0), axis=1)
        return of(counts), of(region_pos)

    w = jnp.arange(WINDOW)
    g, p, x = w // 16, w // 4 % 4, (x_ - w) % 4
    group = jnp.where(g == 0, outer, (outer - 1) % N_OUTER)
    count, place = pick(
        group * 16 + ((y ^ (p % 2)) * N_X + x) * N_CORE + (core ^ (p // 2))
    )
    before = place[None, :] < place[:, None]
    offset = jnp.sum(jnp.where(before, count[None, :], 0), axis=1)
    rank = jnp.sum(before.astype(jnp.int32), axis=1)
    order = jnp.sum(jnp.where(rank[None, :] == w[:, None], w[None, :], 0), axis=1)

    s = jnp.arange(SHARDS)
    q_count, q_place = pick(outer * 16 + (y * N_X + s // 2) * N_CORE + s % 2)
    q_before = q_place[None, :] < q_place[:, None]
    q_offset = jnp.sum(jnp.where(q_before, q_count[None, :], 0), axis=1)
    q_rank = jnp.sum(q_before.astype(jnp.int32), axis=1)
    q_order = jnp.sum(jnp.where(q_rank[None, :] == s[:, None], s[None, :], 0), axis=1)
    q_key = jnp.sum(jnp.where(place[None, :] < q_place[:, None], count[None, :], 0), axis=1)

    start = jnp.arange(TILES)[:, None] * SLOTS
    within = (q_offset[None, :] < start + SLOTS) & (q_offset[None, :] + q_count[None, :] > start)
    end = q_key[None, :] + jnp.minimum(q_count[None, :], start + SLOTS - q_offset[None, :])
    reach = jnp.max(jnp.where(within, end, 0), axis=1)
    tiles = (jnp.sum(q_count) + SLOTS - 1) // SLOTS

    pad = lambda a, n: jnp.pad(a, (0, n - a.shape[0]))
    return jnp.concatenate([
        order, offset, count,
        pad(q_order, 16), pad(q_offset, 16), pad(q_count, 16), pad(q_key, 16), pad(reach, 16),
        tiles[None],
    ]).astype(jnp.int32)


def total(*parts):
    return functools.reduce(jnp.add, [a.astype(F32) for a in parts]).astype(BF16)


def to_x(block, step):
    return lax.ppermute(block, "x", [(i, (i + step) % N_X) for i in range(N_X)])


def to_core(block):
    return lax.ppermute(block, "core", [(0, 1), (1, 0)])


def to_group(block, step, flip):
    route = [
        (i * 2 + y, (i + step) % N_OUTER * 2 + (y ^ flip))
        for i in range(N_OUTER)
        for y in range(N_Y)
    ]
    return lax.ppermute(block, ("outer", "y"), route)


def on_device(queries, keys, values, output_gradient, kept_offset, region_pos):
    x = lax.axis_index("x")
    exchange = functools.partial(lax.all_to_all, split_axis=0, concat_axis=0, tiled=True)
    kv = jnp.stack([keys, values]).transpose(2, 0, 1, 3)
    kv = [lax.dynamic_index_in_dim(kv, (x + k) % N_X, 0, keepdims=False) for k in range(N_X)]
    own = jnp.stack([to_x(kv[k], k) if k else kv[0] for k in range(N_X)])

    def by_head(a):
        return a.transpose(1, 0, 2).reshape(SHARDS, HEADS, SLOTS, WIDTH)

    rows = jnp.stack([by_head(queries), by_head(output_gradient)], axis=1)
    own, rows, kept_offset, region_pos = lax.optimization_barrier(
        (own, rows, kept_offset, region_pos)
    )
    scalars = plan(kept_offset, region_pos)
    own_pair = (own, to_group(own, 0, 1))
    prev_pair = (to_group(own, 1, 0), to_group(own, 1, 1))
    pieces = (
        *own_pair, *(to_core(a) for a in own_pair), *prev_pair, *(to_core(a) for a in prev_pair)
    )

    rows = exchange(rows, QUERY_AXES)
    rows, near, far = attention(scalars, rows, prepare_keys(scalars, pieces))
    far = to_core(far)
    term = lambda g, y: total(near[g, y], far[g, y])
    sums = total(
        term(0, 0),
        to_group(term(0, 1), 0, 1),
        to_group(term(1, 0), -1, 0),
        to_group(term(1, 1), -1, 1),
    )
    grads = [to_x(sums[k], -k) if k else sums[0] for k in range(N_X)]
    home = exchange(rows, QUERY_AXES)

    def by_slot(a):
        return a.reshape(HEADS_Q, SLOTS, WIDTH).transpose(1, 0, 2)

    output, query_gradient = by_slot(home[:, 0]), by_slot(home[:, 1])
    output, query_gradient, grads = lax.optimization_barrier((output, query_gradient, grads))
    grads = jnp.stack([lax.select_n((h - x) % N_X, *grads) for h in range(N_X)])
    return (
        output,
        query_gradient,
        grads[:, 0].transpose(1, 0, 2),
        grads[:, 1].transpose(1, 0, 2),
    )


def solution(mesh):
    devices = mesh.devices.reshape(N_OUTER, N_Y, N_X, N_CORE)
    split = Mesh(devices, ("outer", "y", "x", "core"))
    rows = P(("outer", "y", "x", "core"), None, None)
    return jax.shard_map(
        on_device,
        mesh=split,
        in_specs=(rows, rows, rows, rows, P(), P()),
        out_specs=(rows, rows, rows, rows),
        check_vma=False,
    )
```

```python
import functools
import math

import jax
import jax.numpy as jnp
from jax import lax
from jax.experimental import pallas as pl
from jax.experimental.pallas import tpu as pltpu
from jax.sharding import Mesh
from jax.sharding import PartitionSpec as P

REGION = 1024
SLOTS = 128
WIDTH = 128
HEADS_Q = 32
HEADS_KV = 4
N_OUTER = 16
N_Y = 2
N_X = 4
N_CORE = 2
WINDOW = 32
KEY_ROWS = WINDOW * SLOTS
PIECES = 8

QUERY_AXES = ("x", "core")
SHARDS = N_X * N_CORE
HEADS = HEADS_Q // SHARDS
QUERY_ROWS = SHARDS * SLOTS
TILES = SHARDS
LANES = HEADS * SLOTS
UNIT = 256
SPAN = 512
ONES = 16
UNITS = KEY_ROWS // UNIT
SAFE = 60.0

FILL = -1e30
FLOOR = -1e29
SCALE = WIDTH ** (-0.5)
BASE_TWO = SCALE * math.log2(math.e)
BF16, F32, I32 = jnp.bfloat16, jnp.float32, jnp.int32

KEY_ORDER = 0
KEY_OFFSET = 32
KEY_COUNT = 64
QUERY_ORDER = 96
QUERY_OFFSET = 112
QUERY_COUNT = 128
QUERY_KEY = 144
REACH = 160
CLEAR = 176
TILE_COUNT = 192


def slots():
    return lax.broadcasted_iota(I32, (SLOTS, WIDTH), 0)


def up(n, unit):
    return (n + unit - 1) // unit


def tile_rows(i):
    return pl.ds(pl.multiple_of(i * SLOTS, SLOTS), SLOTS)


def unit_rows(u, rows):
    return pl.ds(pl.multiple_of(u * UNIT, UNIT), rows)


def pack_rows(sc, array, part, packed):
    slot = slots()
    packed[:, tile_rows(sc[TILE_COUNT] - 1), :] = jnp.zeros((HEADS, SLOTS, WIDTH), F32)

    @pl.loop(0, SHARDS)
    def _(j):
        s = sc[QUERY_ORDER + j]
        live = (slot < sc[QUERY_COUNT + s])[None]
        packed[:, pl.ds(sc[QUERY_OFFSET + s], SLOTS), :] = jnp.where(
            live, array[s, part].astype(F32), 0.0
        )


def unpack_rows(sc, packed, array, part):
    slot = slots()

    @pl.loop(0, SHARDS)
    def _(s):
        live = (slot < sc[QUERY_COUNT + s])[None]
        rows = packed[:, pl.ds(sc[QUERY_OFFSET + s], SLOTS), :]
        array[s, part] = jnp.where(live, rows, 0.0).astype(BF16)


def shown(s, first, limit):
    place = lax.broadcasted_iota(I32, s.shape, 0)
    return jnp.where(place <= limit - first, s, FILL)


def fold(op, s):
    return op(s.reshape(-1, 8, s.shape[1]), axis=0)


def square(a):
    a = a.astype(F32)
    return jnp.sum(a * a, axis=0, keepdims=True)


def prepare(sc, *refs):
    pieces, out_refs, long_ref = refs[:PIECES], refs[PIECES : PIECES + 4], refs[PIECES + 4]
    kc, vc, kt, vt, longs, stage, kf, vf, sems, out_sems = refs[PIECES + 5 :]
    spans = up(sc[REACH + sc[TILE_COUNT] - 1], SPAN)
    copies = [
        pltpu.make_async_copy(ref, stage.at[pl.ds(p * N_X, N_X)], sems.at[p])
        for p, ref in enumerate(pieces)
    ]
    for copy in copies:
        copy.start()
    tail = pl.ds(pl.multiple_of((spans - 1) * SPAN, SPAN), SPAN)
    kf[tail, :] = jnp.zeros((SPAN, WIDTH), F32)
    vf[tail, :] = jnp.zeros((SPAN, WIDTH), F32)
    for copy in copies:
        copy.wait()

    @pl.loop(0, WINDOW)
    def _(j):
        w = sc[KEY_ORDER + j]
        rows = pl.ds(sc[KEY_OFFSET + w], SLOTS)
        kf[rows, :] = stage[w, 0].astype(F32)
        vf[rows, :] = stage[w, 1].astype(F32)

    def turn(n, longest):
        rows = pl.ds(pl.multiple_of(n * SPAN, SPAN), SPAN)
        keys = kf[rows, :].astype(BF16)
        vals = vf[rows, :].astype(BF16)
        kc[rows, :] = keys
        vc[rows, :] = vals
        keys = keys.T
        kt[n] = keys
        vt[n, :WIDTH] = vals.T
        vt[n, WIDTH:] = jnp.ones((ONES, SPAN), BF16)
        return jnp.maximum(longest, square(keys))

    longs[...] = lax.fori_loop(0, spans, turn, jnp.zeros((1, SPAN), F32))
    out_copies = [
        pltpu.make_async_copy(held, ref, out_sems.at[n])
        for n, (held, ref) in enumerate(zip((kc, vc, kt, vt, longs), (*out_refs, long_ref)))
    ]
    for copy in out_copies:
        copy.start()
    for copy in out_copies:
        copy.wait()


def attend(sc, long_ref, rows_ref, *refs):
    keys_refs, (out_ref, *term_refs), scratch = refs[:4], refs[4:7], refs[7:]
    raw, kc, vc, kt, vt, qf, gf, thr, limits, qt, gt, ot, dqt = scratch[:13]
    wb, wn, db, dk, dv, tops, terms, sems, out_sems = scratch[13:]
    slot = slots()
    tiles = sc[TILE_COUNT]

    copies = [
        pltpu.make_async_copy(ref, place, sems.at[n])
        for n, (ref, place) in enumerate(zip((rows_ref, *keys_refs), (raw, kc, vc, kt, vt)))
    ]
    for copy in copies:
        copy.start()

    thr[tile_rows(tiles - 1), :] = jnp.full((SLOTS, WIDTH), -1, I32)

    @pl.loop(0, UNITS)
    def _(u):
        dk[unit_rows(u, UNIT), :] = jnp.zeros((UNIT, WIDTH), F32)
        dv[unit_rows(u, UNIT), :] = jnp.zeros((UNIT, WIDTH), F32)

    @pl.loop(0, SHARDS)
    def _(j):
        s = sc[QUERY_ORDER + j]
        thr[pl.ds(sc[QUERY_OFFSET + s], SLOTS), :] = jnp.where(
            slot < sc[QUERY_COUNT + s], slot + sc[QUERY_KEY + s], -1
        )

    longest = jnp.max(long_ref[...])
    copies[0].wait()
    pack_rows(sc, raw, 0, qf)
    pack_rows(sc, raw, 1, gf)
    for copy in copies[1:]:
        copy.wait()

    def turn(i, longest_row):
        rows = tile_rows(i)
        limits[i] = jnp.concatenate([thr[rows, :].T[0:1, :]] * HEADS, axis=1)
        q_turn = qf[:, rows, :].astype(BF16).reshape(LANES, WIDTH).T
        qt[i] = q_turn
        gt[i] = gf[:, rows, :].astype(BF16).reshape(LANES, WIDTH).T
        return jnp.maximum(longest_row, square(q_turn))

    longest_row = jnp.max(lax.fori_loop(0, tiles, turn, jnp.zeros((1, LANES), F32)))
    safe = longest_row * longest * BASE_TWO ** 2 <= SAFE ** 2

    def span_rows(n):
        return pl.ds(pl.multiple_of(n * SPAN, SPAN), SPAN)

    def scores(i, n, masked=True):
        s = jnp.dot(kc[span_rows(n), :], qt[i], preferred_element_type=F32)
        return shown(s, n * SPAN, limits[i]) if masked else s

    def weigh(i, n, masked=True):
        w = jnp.exp2(scores(i, n, masked) * BASE_TWO - tops[i]).astype(BF16)
        wb[span_rows(n), :] = w
        wn[...] = w

    @pl.loop(0, tiles)
    def _(i):
        top = lax.fori_loop(
            0,
            jnp.where(safe, 0, up(sc[REACH + i], SPAN)),
            lambda n, top: jnp.maximum(top, fold(jnp.max, scores(i, n))),
            jnp.full((8, LANES), jnp.where(safe, 0.0, FLOOR), F32),
        )
        top = jnp.max(top, axis=0, keepdims=True)
        tops[i] = jnp.where(top > FLOOR, top, 0.0) * BASE_TWO

    weigh(0, 0)

    @pl.loop(0, tiles)
    def _(i):
        rows = tile_rows(i)
        count = up(sc[REACH + i], SPAN)
        clear = jnp.maximum(sc[CLEAR + i], 1)

        def mix(n):
            return jnp.dot(vt[n], wn[...], preferred_element_type=F32)

        def step(masked, n, acc):
            acc = acc + mix(n - 1)
            weigh(i, n, masked)
            return acc

        acc = jnp.zeros((WIDTH + ONES, LANES), F32)
        acc = lax.fori_loop(1, clear, functools.partial(step, False), acc)
        acc = lax.fori_loop(clear, count, functools.partial(step, True), acc)
        acc = acc + mix(count - 1)
        acc, total = acc[:WIDTH], acc[WIDTH : WIDTH + 1]
        inverse = 1.0 / jnp.where(total > 0.0, total, 1.0)
        out = (acc * inverse).astype(BF16)
        ot[i] = out

        g_turn = gt[i]
        delta = jnp.sum(g_turn.astype(F32) * out.astype(F32), axis=0, keepdims=True)
        by_row = jnp.stack([
            jnp.broadcast_to(inverse[:, h * SLOTS : (h + 1) * SLOTS], (SLOTS, SLOTS)).T
            for h in range(HEADS)
        ])
        q_tile = (qf[:, rows, :] * by_row).astype(BF16).reshape(LANES, WIDTH)
        g_tile = (gf[:, rows, :] * by_row).astype(BF16).reshape(LANES, WIDTH)

        def weigh_back(n):
            at = span_rows(n)
            dp = jnp.dot(vc[at, :], g_turn, preferred_element_type=F32)
            db[...] = (wb[at, :].astype(F32) * (dp - delta)).astype(BF16)

        def mix_back(n, acc):
            at = span_rows(n)
            dv[at, :] += jnp.dot(wb[at, :], g_tile, preferred_element_type=F32)
            dk[at, :] += jnp.dot(db[...], q_tile, preferred_element_type=F32)
            return acc + jnp.dot(kt[n], db[...], preferred_element_type=F32)

        def step_back(n, acc):
            acc = mix_back(n - 1, acc)
            weigh_back(n)
            return acc

        weigh_back(0)
        acc = lax.fori_loop(1, count, step_back, jnp.zeros((WIDTH, LANES), F32))
        acc = mix_back(count - 1, acc)
        dqt[i] = (acc * (inverse * SCALE)).astype(BF16)
        weigh(jnp.minimum(i + 1, tiles - 1), 0)

    out_copies = [
        pltpu.make_async_copy(terms.at[far], term_refs[far], out_sems.at[far]) for far in range(2)
    ]
    out_copies += [
        pltpu.make_async_copy(raw.at[:, part], out_ref.at[:, part], out_sems.at[2 + part])
        for part in range(2)
    ]
    for far in range(2):
        for g in range(2):

            @pl.loop(0, 2 * N_X)
            def _(e, g=g, far=far):
                y, x = e // N_X, e % N_X
                w = g * 16 + far * 8 + e
                rows = pl.ds(sc[KEY_OFFSET + w], SLOTS)
                live = slot < sc[KEY_COUNT + w]
                terms[far, g, y, x, 0] = jnp.where(live, dk[rows, :] * SCALE, 0.0).astype(BF16)
                terms[far, g, y, x, 1] = jnp.where(live, dv[rows, :], 0.0).astype(BF16)

        out_copies[far].start()

    for part, (turned, packed) in enumerate(((ot, qf), (dqt, gf))):

        @pl.loop(0, tiles)
        def _(i, turned=turned, packed=packed):
            rows = turned[i].T.astype(F32).reshape(HEADS, SLOTS, WIDTH)
            packed[:, tile_rows(i), :] = rows

        unpack_rows(sc, packed, raw, part)
        out_copies[2 + part].start()

    for copy in out_copies:
        copy.wait()


ROWS = (SHARDS, 2, HEADS, SLOTS, WIDTH)
KEYS = (KEY_ROWS, WIDTH)
TURNED_KEYS = (KEY_ROWS // SPAN, WIDTH, SPAN)
TURNED_VALUES = (KEY_ROWS // SPAN, WIDTH + ONES, SPAN)
PACKING_KEYS = pltpu.VMEM((KEY_ROWS + SLOTS, WIDTH), F32)
PACKING_ROWS = pltpu.VMEM((HEADS, QUERY_ROWS + SLOTS, WIDTH), F32)


def call(kernel, operands, spaces, out_shape, out_space, scratch, flops, limit, name):
    return pl.pallas_call(
        kernel,
        out_shape=out_shape,
        in_specs=[pl.BlockSpec(memory_space=space) for space in spaces],
        out_specs=(pl.BlockSpec(memory_space=out_space),) * len(out_shape),
        scratch_shapes=scratch,
        compiler_params=pltpu.CompilerParams(vmem_limit_bytes=limit << 20),
        cost_estimate=pl.CostEstimate(flops=flops, bytes_accessed=6 << 20, transcendentals=0),
        name=name,
    )(*operands)


def prepare_keys(scalars, pieces):
    shape = jax.ShapeDtypeStruct
    return call(
        prepare,
        (scalars, *pieces),
        (pltpu.SMEM,) + (pltpu.HBM,) * PIECES,
        (
            shape(KEYS, BF16),
            shape(KEYS, BF16),
            shape(TURNED_KEYS, BF16),
            shape(TURNED_VALUES, BF16),
            shape((1, SPAN), F32),
        ),
        pltpu.HBM,
        [
            *[pltpu.VMEM(KEYS, BF16)] * 2,
            pltpu.VMEM(TURNED_KEYS, BF16),
            pltpu.VMEM(TURNED_VALUES, BF16),
            pltpu.VMEM((1, SPAN), F32),
            pltpu.VMEM((WINDOW, 2, SLOTS, WIDTH), BF16),
            PACKING_KEYS,
            PACKING_KEYS,
            pltpu.SemaphoreType.DMA((PIECES,)),
            pltpu.SemaphoreType.DMA((5,)),
        ],
        1 << 20,
        56,
        "window_keys",
    )


def attention(scalars, rows, packed):
    *keys, longest = packed
    terms = jax.ShapeDtypeStruct((2, 2, N_X, 2, SLOTS, WIDTH), BF16)
    return call(
        attend,
        (scalars, longest, rows, *keys),
        (pltpu.SMEM, pltpu.VMEM, pl.ANY) + (pltpu.HBM,) * 4,
        (jax.ShapeDtypeStruct(ROWS, BF16), terms, terms),
        pltpu.HBM,
        [
            pltpu.VMEM(ROWS, BF16),
            *[pltpu.VMEM(KEYS, BF16)] * 2,
            pltpu.VMEM(TURNED_KEYS, BF16),
            pltpu.VMEM(TURNED_VALUES, BF16),
            *[PACKING_ROWS] * 2,
            pltpu.VMEM((QUERY_ROWS + SLOTS, WIDTH), I32),
            pltpu.VMEM((TILES, 1, LANES), I32),
            *[pltpu.VMEM((TILES, WIDTH, LANES), BF16)] * 4,
            pltpu.VMEM((KEY_ROWS, LANES), BF16),
            pltpu.VMEM((SPAN, LANES), BF16),
            pltpu.VMEM((SPAN, LANES), BF16),
            *[PACKING_KEYS] * 2,
            pltpu.VMEM((TILES, 1, LANES), F32),
            pltpu.VMEM((2, *terms.shape), BF16),
            pltpu.SemaphoreType.DMA((5,)),
            pltpu.SemaphoreType.DMA((4,)),
        ],
        20 << 30,
        56,
        "window_attention",
    )


def plan(kept_offset, region_pos):
    outer, y, x_, core = (lax.axis_index(a) for a in ("outer", "y", "x", "core"))
    shard = jnp.arange(N_OUTER * N_Y * N_X * N_CORE)
    counts = jnp.sum((kept_offset < REGION).astype(jnp.int32), axis=1)

    def pick(ids):
        hit = ids[:, None] == shard[None, :]
        of = lambda a: jnp.sum(jnp.where(hit, a[None, :], 0), axis=1)
        return of(counts), of(region_pos)

    w = jnp.arange(WINDOW)
    g, p, x = w // 16, w // 4 % 4, (x_ - w) % 4
    group = jnp.where(g == 0, outer, (outer - 1) % N_OUTER)
    count, place = pick(
        group * 16 + ((y ^ (p % 2)) * N_X + x) * N_CORE + (core ^ (p // 2))
    )
    before = place[None, :] < place[:, None]
    offset = jnp.sum(jnp.where(before, count[None, :], 0), axis=1)
    rank = jnp.sum(before.astype(jnp.int32), axis=1)
    order = jnp.sum(jnp.where(rank[None, :] == w[:, None], w[None, :], 0), axis=1)

    s = jnp.arange(SHARDS)
    q_count, q_place = pick(outer * 16 + (y * N_X + s // 2) * N_CORE + s % 2)
    q_before = q_place[None, :] < q_place[:, None]
    q_offset = jnp.sum(jnp.where(q_before, q_count[None, :], 0), axis=1)
    q_rank = jnp.sum(q_before.astype(jnp.int32), axis=1)
    q_order = jnp.sum(jnp.where(q_rank[None, :] == s[:, None], s[None, :], 0), axis=1)
    q_key = jnp.sum(jnp.where(place[None, :] < q_place[:, None], count[None, :], 0), axis=1)

    start = jnp.arange(TILES)[:, None] * SLOTS
    within = (q_offset[None, :] < start + SLOTS) & (q_offset[None, :] + q_count[None, :] > start)
    end = q_key[None, :] + jnp.minimum(q_count[None, :], start + SLOTS - q_offset[None, :])
    reach = jnp.max(jnp.where(within, end, 0), axis=1)
    first = q_key[None, :] + jnp.maximum(start - q_offset[None, :], 0)
    clear = (jnp.min(jnp.where(within, first, KEY_ROWS), axis=1) + 1) // SPAN
    tiles = (jnp.sum(q_count) + SLOTS - 1) // SLOTS

    pad = lambda a, n: jnp.pad(a, (0, n - a.shape[0]))
    return jnp.concatenate([
        order, offset, count,
        pad(q_order, 16), pad(q_offset, 16), pad(q_count, 16), pad(q_key, 16), pad(reach, 16), pad(clear, 16),
        tiles[None],
    ]).astype(jnp.int32)


def total(*parts):
    return functools.reduce(jnp.add, [a.astype(F32) for a in parts]).astype(BF16)


def to_x(block, step):
    return lax.ppermute(block, "x", [(i, (i + step) % N_X) for i in range(N_X)])


def to_core(block):
    return lax.ppermute(block, "core", [(0, 1), (1, 0)])


def to_group(block, step, flip):
    route = [
        (i * 2 + y, (i + step) % N_OUTER * 2 + (y ^ flip))
        for i in range(N_OUTER)
        for y in range(N_Y)
    ]
    return lax.ppermute(block, ("outer", "y"), route)


def on_device(queries, keys, values, output_gradient, kept_offset, region_pos):
    x = lax.axis_index("x")
    exchange = functools.partial(lax.all_to_all, split_axis=0, concat_axis=0, tiled=True)
    kv = jnp.stack([keys, values]).transpose(2, 0, 1, 3)
    kv = [lax.dynamic_index_in_dim(kv, (x + k) % N_X, 0, keepdims=False) for k in range(N_X)]
    own = jnp.stack([to_x(kv[k], k) if k else kv[0] for k in range(N_X)])

    def by_head(a):
        return a.transpose(1, 0, 2).reshape(SHARDS, HEADS, SLOTS, WIDTH)

    rows = jnp.stack([by_head(queries), by_head(output_gradient)], axis=1)
    own, rows, kept_offset, region_pos = lax.optimization_barrier(
        (own, rows, kept_offset, region_pos)
    )
    scalars = plan(kept_offset, region_pos)
    own_pair = (own, to_group(own, 0, 1))
    prev_pair = (to_group(own, 1, 0), to_group(own, 1, 1))
    pieces = (
        *own_pair, *(to_core(a) for a in own_pair), *prev_pair, *(to_core(a) for a in prev_pair)
    )

    rows = exchange(rows, QUERY_AXES)
    rows, near, far = attention(scalars, rows, prepare_keys(scalars, pieces))
    far = to_core(far)
    term = lambda g, y: total(near[g, y], far[g, y])
    sums = total(
        term(0, 0),
        to_group(term(0, 1), 0, 1),
        to_group(term(1, 0), -1, 0),
        to_group(term(1, 1), -1, 1),
    )
    grads = [to_x(sums[k], -k) if k else sums[0] for k in range(N_X)]
    home = exchange(rows, QUERY_AXES)

    def by_slot(a):
        return a.reshape(HEADS_Q, SLOTS, WIDTH).transpose(1, 0, 2)

    output, query_gradient = by_slot(home[:, 0]), by_slot(home[:, 1])
    output, query_gradient, grads = lax.optimization_barrier((output, query_gradient, grads))
    grads = jnp.stack([lax.select_n((h - x) % N_X, *grads) for h in range(N_X)])
    return (
        output,
        query_gradient,
        grads[:, 0].transpose(1, 0, 2),
        grads[:, 1].transpose(1, 0, 2),
    )


def solution(mesh):
    devices = mesh.devices.reshape(N_OUTER, N_Y, N_X, N_CORE)
    split = Mesh(devices, ("outer", "y", "x", "core"))
    rows = P(("outer", "y", "x", "core"), None, None)
    return jax.shard_map(
        on_device,
        mesh=split,
        in_specs=(rows, rows, rows, rows, P(), P()),
        out_specs=(rows, rows, rows, rows),
        check_vma=False,
    )
```

```python
import functools
import math

import jax
import jax.numpy as jnp
from jax import lax
from jax.experimental import pallas as pl
from jax.experimental.pallas import tpu as pltpu
from jax.sharding import Mesh
from jax.sharding import PartitionSpec as P

REGION = 1024
SLOTS = 128
WIDTH = 128
HEADS_Q = 32
HEADS_KV = 4
N_OUTER = 16
N_Y = 2
N_X = 4
N_CORE = 2
WINDOW = 32
KEY_ROWS = WINDOW * SLOTS
PIECES = 8

QUERY_AXES = ("x", "core")
SHARDS = N_X * N_CORE
HEADS = HEADS_Q // SHARDS
QUERY_ROWS = SHARDS * SLOTS
TILES = SHARDS
LANES = HEADS * SLOTS
UNIT = 256
SPAN = 512
ONES = 16
UNITS = KEY_ROWS // UNIT
SAFE = 60.0

FILL = -1e30
FLOOR = -1e29
SCALE = WIDTH ** (-0.5)
BASE_TWO = SCALE * math.log2(math.e)
BF16, F32, I32 = jnp.bfloat16, jnp.float32, jnp.int32

KEY_ORDER = 0
KEY_OFFSET = 32
KEY_COUNT = 64
QUERY_ORDER = 96
QUERY_OFFSET = 112
QUERY_COUNT = 128
QUERY_KEY = 144
REACH = 160
TILE_COUNT = 176


def slots():
    return lax.broadcasted_iota(I32, (SLOTS, WIDTH), 0)


def up(n, unit):
    return (n + unit - 1) // unit


def tile_rows(i):
    return pl.ds(pl.multiple_of(i * SLOTS, SLOTS), SLOTS)


def unit_rows(u, rows):
    return pl.ds(pl.multiple_of(u * UNIT, UNIT), rows)


def pack_rows(sc, array, part, packed):
    slot = slots()
    packed[:, tile_rows(sc[TILE_COUNT] - 1), :] = jnp.zeros((HEADS, SLOTS, WIDTH), F32)

    @pl.loop(0, SHARDS)
    def _(j):
        s = sc[QUERY_ORDER + j]
        live = (slot < sc[QUERY_COUNT + s])[None]
        packed[:, pl.ds(sc[QUERY_OFFSET + s], SLOTS), :] = jnp.where(
            live, array[s, part].astype(F32), 0.0
        )


def unpack_rows(sc, packed, array, part):
    slot = slots()

    @pl.loop(0, SHARDS)
    def _(s):
        live = (slot < sc[QUERY_COUNT + s])[None]
        rows = packed[:, pl.ds(sc[QUERY_OFFSET + s], SLOTS), :]
        array[s, part] = jnp.where(live, rows, 0.0).astype(BF16)


def shown(s, first, limit):
    place = lax.broadcasted_iota(I32, s.shape, 0)
    return jnp.where(place <= limit - first, s, FILL)


def fold(op, s):
    return op(s.reshape(-1, 8, s.shape[1]), axis=0)


def square(a):
    a = a.astype(F32)
    return jnp.sum(a * a, axis=0, keepdims=True)


def prepare(sc, *refs):
    pieces, out_refs, long_ref = refs[:PIECES], refs[PIECES : PIECES + 4], refs[PIECES + 4]
    kc, vc, kt, vt, longs, stage, kf, vf, sems, out_sems = refs[PIECES + 5 :]
    spans = up(sc[REACH + sc[TILE_COUNT] - 1], SPAN)
    copies = [
        pltpu.make_async_copy(ref, stage.at[pl.ds(p * N_X, N_X)], sems.at[p])
        for p, ref in enumerate(pieces)
    ]
    for copy in copies:
        copy.start()
    tail = pl.ds(pl.multiple_of((spans - 1) * SPAN, SPAN), SPAN)
    kf[tail, :] = jnp.zeros((SPAN, WIDTH), F32)
    vf[tail, :] = jnp.zeros((SPAN, WIDTH), F32)
    for copy in copies:
        copy.wait()

    @pl.loop(0, WINDOW)
    def _(j):
        w = sc[KEY_ORDER + j]
        rows = pl.ds(sc[KEY_OFFSET + w], SLOTS)
        kf[rows, :] = stage[w, 0].astype(F32)
        vf[rows, :] = stage[w, 1].astype(F32)

    def turn(n, longest):
        rows = pl.ds(pl.multiple_of(n * SPAN, SPAN), SPAN)
        keys = kf[rows, :].astype(BF16)
        vals = vf[rows, :].astype(BF16)
        kc[rows, :] = keys
        vc[rows, :] = vals
        keys = keys.T
        kt[n] = keys
        vt[n, :WIDTH] = vals.T
        vt[n, WIDTH:] = jnp.ones((ONES, SPAN), BF16)
        return jnp.maximum(longest, square(keys))

    longs[...] = lax.fori_loop(0, spans, turn, jnp.zeros((1, SPAN), F32))
    out_copies = [
        pltpu.make_async_copy(held, ref, out_sems.at[n])
        for n, (held, ref) in enumerate(zip((kc, vc, kt, vt, longs), (*out_refs, long_ref)))
    ]
    for copy in out_copies:
        copy.start()
    for copy in out_copies:
        copy.wait()


def attend(sc, long_ref, rows_ref, *refs):
    keys_refs, (out_ref, *term_refs), scratch = refs[:4], refs[4:7], refs[7:]
    raw, kc, vc, kt, vt, qf, gf, thr, limits, qt, gt, ot, dqt = scratch[:13]
    wb, wn, db, dk, dv, tops, terms, sems, out_sems = scratch[13:]
    slot = slots()
    tiles = sc[TILE_COUNT]

    copies = [
        pltpu.make_async_copy(ref, place, sems.at[n])
        for n, (ref, place) in enumerate(zip((rows_ref, *keys_refs), (raw, kc, vc, kt, vt)))
    ]
    for copy in copies:
        copy.start()

    thr[tile_rows(tiles - 1), :] = jnp.full((SLOTS, WIDTH), -1, I32)

    @pl.loop(0, UNITS)
    def _(u):
        dk[unit_rows(u, UNIT), :] = jnp.zeros((UNIT, WIDTH), F32)
        dv[unit_rows(u, UNIT), :] = jnp.zeros((UNIT, WIDTH), F32)

    @pl.loop(0, SHARDS)
    def _(j):
        s = sc[QUERY_ORDER + j]
        thr[pl.ds(sc[QUERY_OFFSET + s], SLOTS), :] = jnp.where(
            slot < sc[QUERY_COUNT + s], slot + sc[QUERY_KEY + s], -1
        )

    longest = jnp.max(long_ref[...])
    copies[0].wait()
    pack_rows(sc, raw, 0, qf)
    pack_rows(sc, raw, 1, gf)
    for copy in copies[1:]:
        copy.wait()

    def turn(i, longest_row):
        rows = tile_rows(i)
        limits[i] = jnp.concatenate([thr[rows, :].T[0:1, :]] * HEADS, axis=1)
        q_turn = qf[:, rows, :].astype(BF16).reshape(LANES, WIDTH).T
        qt[i] = q_turn
        gt[i] = gf[:, rows, :].astype(BF16).reshape(LANES, WIDTH).T
        return jnp.maximum(longest_row, square(q_turn))

    longest_row = jnp.max(lax.fori_loop(0, tiles, turn, jnp.zeros((1, LANES), F32)))
    safe = longest_row * longest * BASE_TWO ** 2 <= SAFE ** 2

    def span_rows(n):
        return pl.ds(pl.multiple_of(n * SPAN, SPAN), SPAN)

    def scores(i, n):
        s = jnp.dot(kc[span_rows(n), :], qt[i], preferred_element_type=F32)
        return shown(s, n * SPAN, limits[i])

    def weigh(i, n):
        w = jnp.exp2(scores(i, n) * BASE_TWO - tops[i]).astype(BF16)
        wb[span_rows(n), :] = w
        wn[...] = w

    @pl.loop(0, tiles)
    def _(i):
        top = lax.fori_loop(
            0,
            jnp.where(safe, 0, up(sc[REACH + i], SPAN)),
            lambda n, top: jnp.maximum(top, fold(jnp.max, scores(i, n))),
            jnp.full((8, LANES), jnp.where(safe, 0.0, FLOOR), F32),
        )
        top = jnp.max(top, axis=0, keepdims=True)
        tops[i] = jnp.where(top > FLOOR, top, 0.0) * BASE_TWO

    weigh(0, 0)

    @pl.loop(0, tiles)
    def _(i):
        rows = tile_rows(i)
        count = up(sc[REACH + i], SPAN)

        def mix(n):
            return jnp.dot(vt[n], wn[...], preferred_element_type=F32)

        def step(n, acc):
            acc = acc + mix(n - 1)
            weigh(i, n)
            return acc

        acc = jnp.zeros((WIDTH + ONES, LANES), F32)
        acc = lax.fori_loop(1, count, step, acc)
        acc = acc + mix(count - 1)
        acc, total = acc[:WIDTH], acc[WIDTH : WIDTH + 1]
        inverse = 1.0 / jnp.where(total > 0.0, total, 1.0)
        out = (acc * inverse).astype(BF16)
        ot[i] = out

        g_turn = gt[i]
        delta = jnp.sum(g_turn.astype(F32) * out.astype(F32), axis=0, keepdims=True)
        by_row = jnp.stack([
            jnp.broadcast_to(inverse[:, h * SLOTS : (h + 1) * SLOTS], (SLOTS, SLOTS)).T
            for h in range(HEADS)
        ])
        q_tile = (qf[:, rows, :] * by_row).astype(BF16).reshape(LANES, WIDTH)
        g_tile = (gf[:, rows, :] * by_row).astype(BF16).reshape(LANES, WIDTH)

        def weigh_back(n):
            at = span_rows(n)
            dp = jnp.dot(vc[at, :], g_turn, preferred_element_type=F32)
            db[...] = (wb[at, :].astype(F32) * (dp - delta)).astype(BF16)

        def mix_back(n, acc):
            at = span_rows(n)
            dv[at, :] += jnp.dot(wb[at, :], g_tile, preferred_element_type=F32)
            dk[at, :] += jnp.dot(db[...], q_tile, preferred_element_type=F32)
            return acc + jnp.dot(kt[n], db[...], preferred_element_type=F32)

        def step_back(n, acc):
            acc = mix_back(n - 1, acc)
            weigh_back(n)
            return acc

        weigh_back(0)
        acc = lax.fori_loop(1, count, step_back, jnp.zeros((WIDTH, LANES), F32))
        acc = mix_back(count - 1, acc)
        dqt[i] = (acc * (inverse * SCALE)).astype(BF16)
        weigh(jnp.minimum(i + 1, tiles - 1), 0)

    out_copies = [
        pltpu.make_async_copy(terms.at[far], term_refs[far], out_sems.at[far]) for far in range(2)
    ]
    out_copies += [
        pltpu.make_async_copy(raw.at[:, part], out_ref.at[:, part], out_sems.at[2 + part])
        for part in range(2)
    ]
    for far in range(2):
        for g in range(2):

            @pl.loop(0, 2 * N_X)
            def _(e, g=g, far=far):
                y, x = e // N_X, e % N_X
                w = g * 16 + far * 8 + e
                rows = pl.ds(sc[KEY_OFFSET + w], SLOTS)
                live = slot < sc[KEY_COUNT + w]
                terms[far, g, y, x, 0] = jnp.where(live, dk[rows, :] * SCALE, 0.0).astype(BF16)
                terms[far, g, y, x, 1] = jnp.where(live, dv[rows, :], 0.0).astype(BF16)

        out_copies[far].start()

    for part, (turned, packed) in enumerate(((ot, qf), (dqt, gf))):

        @pl.loop(0, tiles)
        def _(i, turned=turned, packed=packed):
            rows = turned[i].T.astype(F32).reshape(HEADS, SLOTS, WIDTH)
            packed[:, tile_rows(i), :] = rows

        unpack_rows(sc, packed, raw, part)
        out_copies[2 + part].start()

    for copy in out_copies:
        copy.wait()


ROWS = (SHARDS, 2, HEADS, SLOTS, WIDTH)
KEYS = (KEY_ROWS, WIDTH)
TURNED_KEYS = (KEY_ROWS // SPAN, WIDTH, SPAN)
TURNED_VALUES = (KEY_ROWS // SPAN, WIDTH + ONES, SPAN)
PACKING_KEYS = pltpu.VMEM((KEY_ROWS + SLOTS, WIDTH), F32)
PACKING_ROWS = pltpu.VMEM((HEADS, QUERY_ROWS + SLOTS, WIDTH), F32)


def call(kernel, operands, spaces, out_shape, out_space, scratch, flops, limit, name):
    return pl.pallas_call(
        kernel,
        out_shape=out_shape,
        in_specs=[pl.BlockSpec(memory_space=space) for space in spaces],
        out_specs=(pl.BlockSpec(memory_space=out_space),) * len(out_shape),
        scratch_shapes=scratch,
        compiler_params=pltpu.CompilerParams(vmem_limit_bytes=limit << 20),
        cost_estimate=pl.CostEstimate(flops=flops, bytes_accessed=6 << 20, transcendentals=0),
        name=name,
    )(*operands)


def prepare_keys(scalars, pieces):
    shape = jax.ShapeDtypeStruct
    return call(
        prepare,
        (scalars, *pieces),
        (pltpu.SMEM,) + (pltpu.HBM,) * PIECES,
        (
            shape(KEYS, BF16),
            shape(KEYS, BF16),
            shape(TURNED_KEYS, BF16),
            shape(TURNED_VALUES, BF16),
            shape((1, SPAN), F32),
        ),
        pltpu.HBM,
        [
            *[pltpu.VMEM(KEYS, BF16)] * 2,
            pltpu.VMEM(TURNED_KEYS, BF16),
            pltpu.VMEM(TURNED_VALUES, BF16),
            pltpu.VMEM((1, SPAN), F32),
            pltpu.VMEM((WINDOW, 2, SLOTS, WIDTH), BF16),
            PACKING_KEYS,
            PACKING_KEYS,
            pltpu.SemaphoreType.DMA((PIECES,)),
            pltpu.SemaphoreType.DMA((5,)),
        ],
        1 << 20,
        56,
        "window_keys",
    )


def attention(scalars, rows, packed):
    *keys, longest = packed
    terms = jax.ShapeDtypeStruct((2, 2, N_X, 2, SLOTS, WIDTH), BF16)
    return call(
        attend,
        (scalars, longest, rows, *keys),
        (pltpu.SMEM, pltpu.VMEM, pl.ANY) + (pltpu.HBM,) * 4,
        (jax.ShapeDtypeStruct(ROWS, BF16), terms, terms),
        pltpu.HBM,
        [
            pltpu.VMEM(ROWS, BF16),
            *[pltpu.VMEM(KEYS, BF16)] * 2,
            pltpu.VMEM(TURNED_KEYS, BF16),
            pltpu.VMEM(TURNED_VALUES, BF16),
            *[PACKING_ROWS] * 2,
            pltpu.VMEM((QUERY_ROWS + SLOTS, WIDTH), I32),
            pltpu.VMEM((TILES, 1, LANES), I32),
            *[pltpu.VMEM((TILES, WIDTH, LANES), BF16)] * 4,
            pltpu.VMEM((KEY_ROWS, LANES), BF16),
            pltpu.VMEM((SPAN, LANES), BF16),
            pltpu.VMEM((SPAN, LANES), BF16),
            *[PACKING_KEYS] * 2,
            pltpu.VMEM((TILES, 1, LANES), F32),
            pltpu.VMEM((2, *terms.shape), BF16),
            pltpu.SemaphoreType.DMA((5,)),
            pltpu.SemaphoreType.DMA((4,)),
        ],
        20 << 30,
        56,
        "window_attention",
    )


def plan(kept_offset, region_pos):
    outer, y, x_, core = (lax.axis_index(a) for a in ("outer", "y", "x", "core"))
    shard = jnp.arange(N_OUTER * N_Y * N_X * N_CORE)
    counts = jnp.sum((kept_offset < REGION).astype(jnp.int32), axis=1)

    def pick(ids):
        hit = ids[:, None] == shard[None, :]
        of = lambda a: jnp.sum(jnp.where(hit, a[None, :], 0), axis=1)
        return of(counts), of(region_pos)

    w = jnp.arange(WINDOW)
    g, p, x = w // 16, w // 4 % 4, (x_ - w) % 4
    group = jnp.where(g == 0, outer, (outer - 1) % N_OUTER)
    count, place = pick(
        group * 16 + ((y ^ (p % 2)) * N_X + x) * N_CORE + (core ^ (p // 2))
    )
    before = place[None, :] < place[:, None]
    offset = jnp.sum(jnp.where(before, count[None, :], 0), axis=1)
    rank = jnp.sum(before.astype(jnp.int32), axis=1)
    order = jnp.sum(jnp.where(rank[None, :] == w[:, None], w[None, :], 0), axis=1)

    s = jnp.arange(SHARDS)
    q_count, q_place = pick(outer * 16 + (y * N_X + s // 2) * N_CORE + s % 2)
    q_before = q_place[None, :] < q_place[:, None]
    q_offset = jnp.sum(jnp.where(q_before, q_count[None, :], 0), axis=1)
    q_rank = jnp.sum(q_before.astype(jnp.int32), axis=1)
    q_order = jnp.sum(jnp.where(q_rank[None, :] == s[:, None], s[None, :], 0), axis=1)
    q_key = jnp.sum(jnp.where(place[None, :] < q_place[:, None], count[None, :], 0), axis=1)

    start = jnp.arange(TILES)[:, None] * SLOTS
    within = (q_offset[None, :] < start + SLOTS) & (q_offset[None, :] + q_count[None, :] > start)
    end = q_key[None, :] + jnp.minimum(q_count[None, :], start + SLOTS - q_offset[None, :])
    reach = jnp.max(jnp.where(within, end, 0), axis=1)
    tiles = (jnp.sum(q_count) + SLOTS - 1) // SLOTS

    pad = lambda a, n: jnp.pad(a, (0, n - a.shape[0]))
    return jnp.concatenate([
        order, offset, count,
        pad(q_order, 16), pad(q_offset, 16), pad(q_count, 16), pad(q_key, 16), pad(reach, 16),
        tiles[None],
    ]).astype(jnp.int32)


def total(*parts):
    return functools.reduce(jnp.add, [a.astype(F32) for a in parts]).astype(BF16)


def to_x(block, step):
    return lax.ppermute(block, "x", [(i, (i + step) % N_X) for i in range(N_X)])


def to_core(block):
    return lax.ppermute(block, "core", [(0, 1), (1, 0)])


def to_group(block, step, flip):
    route = [
        (i * 2 + y, (i + step) % N_OUTER * 2 + (y ^ flip))
        for i in range(N_OUTER)
        for y in range(N_Y)
    ]
    return lax.ppermute(block, ("outer", "y"), route)


def on_device(queries, keys, values, output_gradient, kept_offset, region_pos):
    x = lax.axis_index("x")
    exchange = functools.partial(lax.all_to_all, split_axis=0, concat_axis=0, tiled=True)
    kv = jnp.stack([keys, values]).transpose(2, 0, 1, 3)
    kv = [lax.dynamic_index_in_dim(kv, (x + k) % N_X, 0, keepdims=False) for k in range(N_X)]
    own = jnp.stack([to_x(kv[k], k) if k else kv[0] for k in range(N_X)])

    def by_head(a):
        return a.transpose(1, 0, 2).reshape(SHARDS, HEADS, SLOTS, WIDTH)

    rows = jnp.stack([by_head(queries), by_head(output_gradient)], axis=1)
    own, rows, kept_offset, region_pos = lax.optimization_barrier(
        (own, rows, kept_offset, region_pos)
    )
    scalars = plan(kept_offset, region_pos)
    own_pair = (own, to_group(own, 0, 1))
    prev_pair = (to_group(own, 1, 0), to_group(own, 1, 1))
    pieces = (
        *own_pair, *(to_core(a) for a in own_pair), *prev_pair, *(to_core(a) for a in prev_pair)
    )

    rows = exchange(rows, QUERY_AXES)
    rows, near, far = attention(scalars, rows, prepare_keys(scalars, pieces))
    far = to_core(far)
    term = lambda g, y: total(near[g, y], far[g, y])
    sums = total(
        term(0, 0),
        to_group(term(0, 1), 0, 1),
        to_group(term(1, 0), -1, 0),
        to_group(term(1, 1), -1, 1),
    )
    grads = [to_x(sums[k], -k) if k else sums[0] for k in range(N_X)]
    home = exchange(rows, QUERY_AXES)

    def by_slot(a):
        return a.reshape(HEADS_Q, SLOTS, WIDTH).transpose(1, 0, 2)

    output, query_gradient = by_slot(home[:, 0]), by_slot(home[:, 1])
    output, query_gradient, grads = lax.optimization_barrier((output, query_gradient, grads))
    grads = jnp.stack([lax.select_n((h - x) % N_X, *grads) for h in range(N_X)])
    return (
        output,
        query_gradient,
        grads[:, 0].transpose(1, 0, 2),
        grads[:, 1].transpose(1, 0, 2),
    )


def solution(mesh):
    devices = mesh.devices.reshape(N_OUTER, N_Y, N_X, N_CORE)
    split = Mesh(devices, ("outer", "y", "x", "core"))
    rows = P(("outer", "y", "x", "core"), None, None)
    return jax.shard_map(
        on_device,
        mesh=split,
        in_specs=(rows, rows, rows, rows, P(), P()),
        out_specs=(rows, rows, rows, rows),
        check_vma=False,
    )
```
